512 devices in a mesh: seq: 64 (over y, x, z_lo), head: 8 (over z_hi, core).
Axes of the slice: x: 4, y: 4, z: 16 (z_hi: 4, z_lo: 4; z = z_hi * 4 + z_lo), core: 2. Of those that a mesh axis runs over, the one named last changes fastest.
Arguments:
- queries: bfloat16 [16384, 5120], P('seq', 'head'), may hold values from -100 to 100
- keys: bfloat16 [16384, 5120], P('seq', 'head'), may hold values from -12 to 12
- values: bfloat16 [16384, 5120], P('seq', 'head'), may hold values from -6 to 6
- hidden: bfloat16 [16384, 5120], P('seq', 'head'), may hold values from -3 to 3
- cached: bfloat16 [16384, 5120], P('seq', 'head'), may hold values from -6 to 6
- active: int32 [16384], P('seq'), may hold values from 0 to 1, as said below
- w_out: bfloat16 [5120, 5120], P('head', 'seq'), may hold values from -0.078125 to 0.078125
Outputs:
- block_output: bfloat16 [16384, 5120], P('seq', 'head')
The draws below stay inside these ranges and needn't reach their ends.
Inputs may be any that keep to these rules, and one draw needn't show every extreme that they name: `active`: exactly 704 ones in all; among the 256 tokens of one index of seq at most 32 ones, and that many on some of them.
All inputs are finite; a program needn't handle non-finite values.
Results may differ from the reference program's by a relative error of at most 0.0039.
Values may be sent and summed in bfloat16 or wider, within the bound.
A program may use at most 64 MiB of HBM per device.

```python
import jax
import jax.numpy as jnp
from jax import lax

D = 5120
HEADS = 40
HD = 128
TOK_DEV = 256
TOTAL_ACT = 704
TOKENS = 16384


def shared_base(key):
    return 1.6 * jax.random.normal(jax.random.fold_in(key, 11), (TOKENS, D), jnp.float32)


def draw_keys(key, part):
    result = shared_base(key)
    return jnp.clip(result, -12.0, 12.0).astype(jnp.bfloat16)


def draw_queries(key, part):
    result = 1.6 * jax.random.normal(jax.random.fold_in(key, 13), (TOKENS, D), jnp.float32)
    return jnp.clip(result, -100.0, 100.0).astype(jnp.bfloat16)


def draw_active(key, part):
    blocks = TOKENS // TOK_DEV
    capacity = TOK_DEV // 8
    device_order = jax.random.permutation(jax.random.fold_in(key, 3), blocks)
    counts = jnp.where(device_order < blocks // 8, capacity, capacity // 4)
    subkeys = jax.random.split(jax.random.fold_in(key, 5), blocks)
    ranking = jax.vmap(lambda subkey: jax.random.permutation(subkey, TOK_DEV))(subkeys)
    return (ranking < counts[:, None]).astype(jnp.int32).reshape(TOKENS)


def level_of(rng, shape, shards, least, top_value):
    def one(axis_at, blocks):
        heights = jax.random.uniform(jax.random.fold_in(jax.random.fold_in(rng, 6), axis_at), (blocks,), jnp.float32, least / len(shards), top_value / len(shards))
        return jnp.repeat(jnp.exp(heights), shape[axis_at] // blocks).reshape((-1,) + (1,) * (len(shape) - axis_at - 1))

    factor_of = one(*shards[0])
    for cut in shards[1:]:
        factor_of = factor_of * one(*cut)
    return factor_of


def scatter_about(own_key, shape, deviation, limit, shards=(), kind=jnp.bfloat16):
    values = jax.random.normal(own_key, shape, jnp.float32) * deviation
    if len(shards) > 0:
        values = level_of(own_key, shape, shards, -0.22, 0.18) * values
    return jnp.clip(values, min=-limit, max=limit).astype(kind)


def setup_inputs(seed: int = 0) -> dict:
    key_list = jax.random.split(jax.random.key(seed), 8)
    queries = draw_queries(jax.random.fold_in(key_list[7], 71), 0)
    keys = draw_keys(jax.random.fold_in(key_list[7], 71), 0)
    values = scatter_about(key_list[2], (TOKENS, D), 1.0, 6.0, ((0, 64), (1, 8)))
    hidden = scatter_about(key_list[3], (TOKENS, D), 0.5, 3.0, ((0, 64), (1, 8)))
    cached = scatter_about(key_list[4], (TOKENS, D), 1.0, 6.0, ((0, 64), (1, 8)))
    active = draw_active(jax.random.fold_in(key_list[7], 71), 0)
    w_out = scatter_about(key_list[6], (D, D), D ** -0.5, 0.078125, ((0, 8), (1, 64)))
    return dict(queries=queries, keys=keys, values=values, hidden=hidden, cached=cached, active=active, w_out=w_out)


def reference(queries, keys, values, hidden, cached, active, w_out):
    act_rows = jnp.nonzero(active, size=TOTAL_ACT, fill_value=0)[0].astype(jnp.int32)
    picked = queries[act_rows]
    blocks = TOKENS // TOK_DEV
    inv_root = 1.0 / (HD ** 0.5)

    def one_head(head):
        start = head * HD
        q_head = lax.dynamic_slice_in_dim(picked, start, HD, 1)
        k_head = lax.dynamic_slice_in_dim(keys, start, HD, 1)
        v_head = lax.dynamic_slice_in_dim(values, start, HD, 1)
        scores = jnp.dot(q_head, k_head.T, preferred_element_type=jnp.float32) * inv_root
        scores = scores.reshape(TOTAL_ACT, blocks, TOK_DEV)
        peak = jnp.max(scores, axis=2)
        expo = jnp.exp(scores - peak[:, :, None])
        total = jnp.sum(expo, axis=2)
        probs = expo.astype(jnp.bfloat16)
        partial_out = jnp.einsum("anb,nbd->and", probs.astype(jnp.float32),
                                 v_head.reshape(blocks, TOK_DEV, HD).astype(jnp.float32))
        partial_out = (partial_out / total[:, :, None]).astype(jnp.bfloat16)
        top_max = jnp.max(peak, axis=1, keepdims=True)
        weight = total * jnp.exp(peak - top_max)
        mixed = jnp.einsum("an,and->ad", weight, partial_out.astype(jnp.float32))
        return mixed / jnp.sum(weight, axis=1)[:, None]

    per_head = lax.map(one_head, jnp.arange(HEADS, dtype=jnp.int32))
    attn = jnp.transpose(per_head, (1, 0, 2)).reshape(TOTAL_ACT, D).astype(jnp.bfloat16)
    proj = jnp.dot(attn, w_out, preferred_element_type=jnp.float32)
    updated = (hidden[act_rows].astype(jnp.float32) + proj).astype(jnp.bfloat16)
    return cached.at[act_rows].set(updated)
```

```python
import jax
import jax.numpy as jnp
from jax import lax
from jax.experimental import pallas as pl
from jax.experimental.pallas import tpu as pltpu
from jax.sharding import PartitionSpec as P

X, Y, Z, H = 4, 4, 4, 8
HD = 128
CAP = 32
CR = 48
BF = jnp.bfloat16
F32 = jnp.float32
NA, NB = 3, 2
MESH = pl.DeviceIdType.MESH


def log2(n):
    return n.bit_length() - 1


def iota(shape, dim):
    return lax.broadcasted_iota(jnp.int32, shape, dim)


def onehot(cond):
    return jnp.where(cond, 1.0, 0.0).astype(BF)


def mm(a, b):
    return jnp.dot(a, b, preferred_element_type=F32)


def mm_nt(a, b):
    return lax.dot_general(a, b, (((1,), (1,)), ((), ())), preferred_element_type=F32)


def pack_stat(tile):
    lane = iota(tile.shape, 1)
    hi = tile.astype(BF).astype(F32)
    rest = tile - hi
    mid = rest.astype(BF).astype(F32)
    low = rest - mid
    return jnp.where(lane < 8, hi, jnp.where(lane < 16, mid, jnp.where(lane < 24, low, 0.0))).astype(BF)


def merge(sources, heads, sel):
    width = heads * HD
    logs = [mm(s[:, width:], sel[:, :width]) for s in sources]
    top = logs[0]
    for part in logs[1:]:
        top = jnp.maximum(top, part)
    total, mixed = None, None
    for s, part in zip(sources, logs):
        w = jnp.exp(part - top)
        term = w * s[:, :width].astype(F32)
        total = w if total is None else total + w
        mixed = term if mixed is None else mixed + term
    return mixed / total, top + jnp.log(total)


def stat_of(logs, heads):
    lane = iota((logs.shape[0], HD), 1)
    tile = jnp.zeros((logs.shape[0], HD), F32)
    for h in range(heads):
        tile = jnp.where((lane & 7) == h, logs[:, h * HD : (h + 1) * HD], tile)
    return pack_stat(tile)


def body(
    q_ref, k_ref, v_ref, hid_ref, cac_ref, act_ref, w_ref, out_ref,
    qa, qb, cnt, wt, qc, sel, rsel, expand,
    pa, pb, ra, rb, a2, b2, ra2, rb2, a3, b3, ra3, rb3,
    ht, hr, fin, zs, zr, send_sem, recv_sem,
):
    tok, feat = q_ref.shape
    wc = w_ref.shape[1]
    half = NA * HD
    bs_a, bs_b = Y * Z * 16, X * Z * 16
    nr = Y * X * CR
    me, h = lax.axis_index("seq"), lax.axis_index("head")
    z = me & (Z - 1)
    x = (me >> log2(Z)) & (X - 1)
    y = me >> log2(Z * X)

    def xp(d):
        return (y * X + ((x + d) & (X - 1))) * Z + z, h

    def yp(d):
        return (((y + d) & (Y - 1)) * X + x) * Z + z, h

    def zp(d):
        return (y * X + x) * Z + ((z + d) & (Z - 1)), h

    def hp(d):
        return me, (h + d) & (H - 1)

    barrier = pltpu.get_barrier_semaphore()
    peers = (
        [xp(d) for d in range(1, X)] + [yp(d) for d in range(1, Y)] + [zp(d) for d in range(1, Z)] + [hp(d) for d in range(1, H)]
    )
    for p in peers:
        pl.semaphore_signal(barrier, inc=1, device_id=p, device_id_type=MESH)

    counter = [0]

    def copies(make, peer, n):
        found = []
        for d in range(1, n):
            i = counter[0]
            counter[0] += 1
            src, dst = make(d)
            found.append(
                pltpu.make_async_remote_copy(
                    src_ref=src, dst_ref=dst, send_sem=send_sem.at[i], recv_sem=recv_sem.at[i],
                    device_id=peer(d), device_id_type=MESH,
                )
            )
        return found

    every = []

    def start(cs):
        for c in cs:
            c.start()
        every.extend(cs)

    def arrive(cs):
        for c in cs:
            c.wait_recv()

    act = act_ref[...]
    act8 = jnp.broadcast_to(act, (8, tok)).astype(F32).astype(BF)
    before = onehot(iota((tok, tok), 0) < iota((tok, tok), 1))
    rank = mm(act8, before)[0:1, :]
    pick = onehot((iota((CAP, tok), 0).astype(F32) == rank) & (act > 0))
    own = mm(pick, q_ref[...]).astype(BF)
    qa[x, y, z] = own[0:16]
    qb[y, x, z] = own[16:32]
    total = jnp.sum(act.astype(F32), axis=1, keepdims=True)
    cnt[x, y, z] = jnp.where(iota((1, HD), 1) == me, total, 0.0)
    eye = onehot(iota((wc, wc), 0) == iota((wc, wc), 1))
    wt[y, x] = mm_nt(eye, w_ref[...]).astype(BF)

    pl.semaphore_wait(barrier, len(peers))

    cz = copies(lambda d: (cnt.at[x, y, z],) * 2, zp, Z)
    az = copies(lambda d: (qa.at[x, y, z],) * 2, zp, Z)
    bz = copies(lambda d: (qb.at[y, x, z],) * 2, zp, Z)
    start(cz)
    start(az)
    start(bz)
    w0 = pl.ds(0, half)
    w1 = pl.ds(half, feat - half)
    wx0 = copies(lambda d: (wt.at[y, x, :, w0],) * 2, xp, X)
    wy1 = copies(lambda d: (wt.at[y, x, :, w1],) * 2, yp, Y)
    start(wx0)
    start(wy1)

    expand[...] = mm_nt(onehot(iota((tok, tok), 0) == iota((tok, tok), 1)), pick).astype(BF)
    lane, col = iota((HD, half), 0), iota((HD, half), 1)
    sel[...] = onehot(((lane & 7) == (col >> log2(HD))) & (lane < 24))
    ht[...] = jnp.zeros_like(ht)

    cy = copies(lambda d: (cnt.at[x, y],) * 2, yp, Y)
    ay = copies(lambda d: (qa.at[x, y],) * 2, yp, Y)
    bx = copies(lambda d: (qb.at[y, x],) * 2, xp, X)
    arrive(cz)
    start(cy)
    arrive(az)
    start(ay)
    arrive(bz)
    start(bx)
    cx = copies(lambda d: (cnt.at[x],) * 2, xp, X)
    ax = copies(lambda d: (qa.at[x],) * 2, xp, X)
    by = copies(lambda d: (qb.at[y],) * 2, yp, Y)
    arrive(cy)
    start(cx)
    arrive(ay)
    start(ax)
    arrive(bx)
    start(by)
    arrive(cx)

    counts = jnp.sum(cnt[...].reshape(X * Y * Z, HD), axis=0, keepdims=True)
    cnt8 = jnp.broadcast_to(counts, (8, HD)).astype(BF)

    def positions(part, block, size):
        j = iota((HD, size), 1)
        zz = (j >> 4) & (Z - 1)
        o = j >> (4 + log2(Z))
        s = ((o * X + block) if part == 0 else (block * X + o)) * Z + zz
        b = iota((HD, size), 0)
        off = mm(cnt8, onehot(b < s))[0:1, :]
        n = mm(cnt8, onehot(b == s))[0:1, :]
        r = ((j[0:1, :] & 15) + 16 * part).astype(F32)
        return jnp.where(r < n, off + r, -1.0)

    def compact(part, block, size, rows, first):
        pos = positions(part, block, size)

        @pl.loop(0, Y)
        def _(yb):
            i = iota((X * CR, size), 0) + yb * (X * CR)
            got = mm(onehot(i.astype(F32) == pos), rows).astype(BF)
            qc[yb] = got if first else qc[yb] + got

    compact(0, x, bs_a, qa[x].reshape(bs_a, feat), True)
    compact(1, y, bs_b, qb[y].reshape(bs_b, feat), False)
    slot, b = iota((Z * CAP, HD), 0), iota((Z * CAP, HD), 1)
    off = mm_nt(onehot(b < (y * X + x) * Z + (slot >> log2(CAP))), cnt8)[:, 0:1]
    want = off + (slot[:, 0:1] & (CAP - 1)).astype(F32)
    rsel[...] = onehot(iota((Z * CAP, nr), 1).astype(F32) == want)

    for d in range(1, max(X, Y)):
        if d < X:
            arrive(ax[d - 1 : d])
            xb = (x - d) & (X - 1)
            compact(0, xb, bs_a, qa[xb].reshape(bs_a, feat), False)
        if d < Y:
            arrive(by[d - 1 : d])
            yb = (y - d) & (Y - 1)
            compact(1, yb, bs_b, qb[yb].reshape(bs_b, feat), False)

    wy0 = copies(lambda d: (wt.at[y, :, :, w0],) * 2, yp, Y)
    wx1 = copies(lambda d: (wt.at[:, x, :, w1],) * 2, xp, X)
    arrive(wx0)
    start(wy0)
    arrive(wy1)
    start(wx1)

    scale = 1.0 / HD**0.5

    def attend(first, heads, dest):
        @pl.loop(0, Y)
        def _(yb):
            lane = iota((X * CR, HD), 1)
            tile = jnp.zeros((X * CR, HD), F32)
            for i in range(heads):
                c = slice((first + i) * HD, (first + i + 1) * HD)
                score = mm_nt(qc[yb, :, c], k_ref[:, c]) * scale
                peak = jnp.max(score, axis=1, keepdims=True)
                expo = jnp.exp(score - peak)
                total = jnp.sum(expo, axis=1, keepdims=True)
                part = mm(expo.astype(BF), v_ref[:, c]) / total
                dest[yb, :, :, i * HD : (i + 1) * HD] = part.astype(BF).reshape(X, CR, HD)
                tile = jnp.where((lane & 7) == i, peak + jnp.log(total), tile)
            dest[yb, :, :, heads * HD :] = pack_stat(tile).reshape(X, CR, HD)

    attend(0, NA, pa)
    sa = copies(lambda d: (pa.at[(y + d) & (Y - 1)], ra.at[d - 1]), yp, Y)
    start(sa)
    attend(NA, NB, pb)
    sb = copies(lambda d: (pb.at[:, (x + d) & (X - 1)], rb.at[d - 1]), xp, X)
    start(sb)

    arrive(sa)

    @pl.loop(0, X)
    def _(i):
        mean, logs = merge([pa[y, i]] + [ra[d, i] for d in range(Y - 1)], NA, sel[...])
        a2[i, :, :half] = mean.astype(BF)
        a2[i, :, half:] = stat_of(logs, NA)

    sa2 = copies(lambda d: (a2.at[(x + d) & (X - 1)], ra2.at[d - 1]), xp, X)
    start(sa2)
    arrive(sb)

    @pl.loop(0, Y)
    def _(i):
        mean, logs = merge([pb[i, x]] + [rb[d, i] for d in range(X - 1)], NB, sel[...])
        b2[i, :, : NB * HD] = mean.astype(BF)
        b2[i, :, NB * HD :] = stat_of(logs, NB)

    sb2 = copies(lambda d: (b2.at[(y + d) & (Y - 1)], rb2.at[d - 1]), yp, Y)
    start(sb2)
    arrive(sa2)
    mean, logs = merge([a2[x]] + [ra2[d] for d in range(X - 1)], NA, sel[...])
    a3[:, :half] = mean.astype(BF)
    a3[:, half:] = stat_of(logs, NA)
    sa3 = copies(lambda d: (a3, ra3.at[d - 1]), zp, Z)
    start(sa3)
    arrive(sb2)
    mean, logs = merge([b2[y]] + [rb2[d] for d in range(Y - 1)], NB, sel[...])
    b3[:, : NB * HD] = mean.astype(BF)
    b3[:, NB * HD :] = stat_of(logs, NB)
    sb3 = copies(lambda d: (b3, rb3.at[d - 1]), zp, Z)
    start(sb3)
    arrive(sa3)
    attn_a = merge([a3[...]] + [ra3[d] for d in range(Z - 1)], NA, sel[...])[0].astype(BF)
    arrive(wy0)
    arrive(wx1)
    arrive(sb3)
    attn_b = merge([b3[...]] + [rb3[d] for d in range(Z - 1)], NB, sel[...])[0].astype(BF)

    pieces = X * Y // H
    for o in range(H):
        yy, xx = o * pieces // X, o * pieces % X
        w_o = wt[yy, xx : xx + pieces].reshape(pieces * wc, feat)
        term = mm_nt(attn_a, w_o[:, :half]) + mm_nt(attn_b, w_o[:, half:])
        ht[o, :, : pieces * wc] = term.astype(BF)
    sh = copies(lambda d: (ht.at[(h + d) & (H - 1)], hr.at[d - 1]), hp, H)
    start(sh)
    proj = ht[h].astype(F32)
    for d in range(1, H):
        arrive(sh[d - 1 : d])
        proj = proj + hr[d - 1].astype(F32)
    fin[y, x] = proj.astype(BF)

    fx = copies(lambda d: (fin.at[y, x],) * 2, xp, X)
    start(fx)
    arrive(fx)
    fy = copies(lambda d: (fin.at[y],) * 2, yp, Y)
    start(fy)
    arrive(fy)
    zs[...] = mm(rsel[...], fin[...].reshape(nr, 2 * HD)).astype(BF).reshape(Z, CAP, 2 * HD)
    sz = copies(lambda d: (zs.at[(z + d) & (Z - 1)], zr.at[d - 1]), zp, Z)
    start(sz)

    def place(rows, zz):
        l, c = iota((2 * HD, feat), 0), iota((2 * HD, feat), 1)
        second = l >= wc
        at = jnp.where(second, Z * wc - wc, 0) + zz * wc + l
        return mm(rows, onehot((c == at) & (l < pieces * wc)))

    rows = place(zs[z], z)
    for d in range(1, Z):
        arrive(sz[d - 1 : d])
        rows = rows + place(zr[d - 1], (z - d) & (Z - 1))
    grown = mm(expand[...], rows.astype(BF))
    live = mm(expand[...], jnp.ones((CAP, feat), BF)) > 0.5
    out_ref[...] = jnp.where(live, hid_ref[...].astype(F32) + grown, cac_ref[...].astype(F32)).astype(BF)
    for c in every:
        c.wait_send()


def shards(queries, keys, values, hidden, cached, active, w_out):
    tok, feat = queries.shape
    wc = w_out.shape[1]
    wa, wb = (NA + 1) * HD, (NB + 1) * HD
    n_copies = 3 * (Z - 1) + 5 * (X - 1) + 5 * (Y - 1) + 2 * (X + Y - 2) + 3 * (Z - 1) + (H - 1) + 3 * (X + Y)
    vmem = pltpu.VMEM
    scratch = [
        vmem((X, Y, Z, 16, feat), BF),
        vmem((Y, X, Z, 16, feat), BF),
        vmem((X, Y, Z, 1, HD), F32),
        vmem((Y, X, wc, feat), BF),
        vmem((Y, X * CR, feat), BF),
        vmem((HD, NA * HD), BF),
        vmem((Z * CAP, Y * X * CR), BF),
        vmem((tok, CAP), BF),
        vmem((Y, X, CR, wa), BF),
        vmem((Y, X, CR, wb), BF),
        vmem((Y - 1, X, CR, wa), BF),
        vmem((X - 1, Y, CR, wb), BF),
        vmem((X, CR, wa), BF),
        vmem((Y, CR, wb), BF),
        vmem((X - 1, CR, wa), BF),
        vmem((Y - 1, CR, wb), BF),
        vmem((CR, wa), BF),
        vmem((CR, wb), BF),
        vmem((Z - 1, CR, wa), BF),
        vmem((Z - 1, CR, wb), BF),
        vmem((H, CR, 2 * HD), BF),
        vmem((H - 1, CR, 2 * HD), BF),
        vmem((Y, X, CR, 2 * HD), BF),
        vmem((Z, CAP, 2 * HD), BF),
        vmem((Z - 1, CAP, 2 * HD), BF),
        pltpu.SemaphoreType.DMA((n_copies,)),
        pltpu.SemaphoreType.DMA((n_copies,)),
    ]
    return pl.pallas_call(
        body,
        out_shape=jax.ShapeDtypeStruct((tok, feat), BF),
        in_specs=[pl.BlockSpec(memory_space=pltpu.VMEM)] * 7,
        out_specs=pl.BlockSpec(memory_space=pltpu.VMEM),
        scratch_shapes=scratch,
        compiler_params=pltpu.CompilerParams(
            collective_id=0, has_side_effects=True, vmem_limit_bytes=48 * 2**20
        ),
    )(queries, keys, values, hidden, cached, active.reshape(1, tok), w_out)


def solution(mesh):
    placed = (
        P("seq", "head"),
        P("seq", "head"),
        P("seq", "head"),
        P("seq", "head"),
        P("seq", "head"),
        P("seq"),
        P("head", "seq"),
    )
    return jax.shard_map(
        shards, mesh=mesh, in_specs=placed, out_specs=P("seq", "head"), check_vma=False
    )
```

```python
import math

import jax
import jax.numpy as jnp
from jax import lax
from jax.experimental import pallas as pl
from jax.experimental.pallas import tpu as pltpu
from jax.sharding import PartitionSpec as P

X, Y, Z, H = 4, 4, 4, 8
HD = 128
CAP = 32
CR = 48
BF = jnp.bfloat16
F32 = jnp.float32
NA, NB = 3, 2
MESH = pl.DeviceIdType.MESH


def log2(n):
    return n.bit_length() - 1


def iota(shape, dim):
    return lax.broadcasted_iota(jnp.int32, shape, dim)


def onehot(cond):
    return jnp.where(cond, 1.0, 0.0).astype(BF)


def log2_of(v):
    return jnp.log(v) * (1.0 / math.log(2.0))


def mm(a, b):
    return jnp.dot(a, b, preferred_element_type=F32)


def mm_nt(a, b):
    return lax.dot_general(a, b, (((1,), (1,)), ((), ())), preferred_element_type=F32)


def pack_stat(tile):
    lane = iota(tile.shape, 1)
    hi = tile.astype(BF).astype(F32)
    rest = tile - hi
    mid = rest.astype(BF).astype(F32)
    low = rest - mid
    return jnp.where(lane < 8, hi, jnp.where(lane < 16, mid, jnp.where(lane < 24, low, 0.0))).astype(BF)


def merge(sources, heads, sel):
    width = heads * HD
    logs = [mm(s[:, width:], sel[:, :width]) for s in sources]
    top = logs[0]
    for part in logs[1:]:
        top = jnp.maximum(top, part)
    total, mixed = None, None
    for s, part in zip(sources, logs):
        w = lax.exp2(part - top)
        term = w * s[:, :width].astype(F32)
        total = w if total is None else total + w
        mixed = term if mixed is None else mixed + term
    return mixed / total, top + log2_of(total)


def stat_of(logs, heads):
    lane = iota((logs.shape[0], HD), 1)
    tile = jnp.zeros((logs.shape[0], HD), F32)
    for h in range(heads):
        tile = jnp.where((lane & 7) == h, logs[:, h * HD : (h + 1) * HD], tile)
    return pack_stat(tile)


def body(
    q_hbm, k_hbm, v_hbm, hid_hbm, cac_hbm, act_hbm, w_hbm, out_ref,
    q_ref, k_ref, v_ref, hid_ref, cac_ref, act_ref,
    qa, qb, cnt, wt, pma, pmb, vx, sel, rsel, expand,
    pa, pb, ra, rb, a2, b2, ra2, rb2, a3, b3, ra3, rb3,
    ht, hr, fin, zs, zr, send_sem, recv_sem, load_sem,
):
    tok, feat = q_ref.shape
    wc = w_hbm.shape[0]
    half = NA * HD
    nr = Y * X * CR
    me, h = lax.axis_index("seq"), lax.axis_index("head")
    z = me & (Z - 1)
    x = (me >> log2(Z)) & (X - 1)
    y = me >> log2(Z * X)

    def xp(d):
        return (y * X + ((x + d) & (X - 1))) * Z + z, h

    def yp(d):
        return (((y + d) & (Y - 1)) * X + x) * Z + z, h

    def zp(d):
        return (y * X + x) * Z + ((z + d) & (Z - 1)), h

    def hp(d):
        return me, (h + d) & (H - 1)

    barrier = pltpu.get_barrier_semaphore()
    peers = (
        [xp(d) for d in range(1, X)] + [yp(d) for d in range(1, Y)] + [zp(d) for d in range(1, Z)] + [hp(d) for d in range(1, H)]
    )
    for p in peers:
        pl.semaphore_signal(barrier, inc=1, device_id=p, device_id_type=MESH)

    loads = [
        pltpu.make_async_copy(src, dst, load_sem.at[i])
        for i, (src, dst) in enumerate(
            [
                (act_hbm, act_ref), (q_hbm, q_ref), (w_hbm, wt.at[y, x]),
                (k_hbm, k_ref), (v_hbm, v_ref), (hid_hbm, hid_ref), (cac_hbm, cac_ref),
            ]
        )
    ]
    for c in loads:
        c.start()

    counter = [0]
    every = []

    def copies(make, peer, n, steps=None):
        found = []
        for d in range(1, n) if steps is None else steps:
            i = counter[0]
            counter[0] += 1
            src, dst = make(d)
            found.append(
                pltpu.make_async_remote_copy(
                    src_ref=src, dst_ref=dst, send_sem=send_sem.at[i], recv_sem=recv_sem.at[i],
                    device_id=peer(d), device_id_type=MESH,
                )
            )
        return found

    def start(cs):
        for c in cs:
            c.start()
        every.extend(cs)

    def arrive(cs):
        for c in cs:
            c.wait_recv()

    def ring(block, peer, n, at):
        direct = copies(lambda d: (block(at, 0, Z),) * 2, peer, n, [1, n - 1] if n > 2 else [1] * (n - 1))
        on = []
        if n > 2:
            on += copies(lambda d: (block((at - 1) & (n - 1), 0, Z // 2),) * 2, peer, n, [1])
            on += copies(lambda d: (block((at + 1) & (n - 1), Z // 2, Z),) * 2, peer, n, [n - 1])
        return direct, on

    loads[0].wait()
    act = act_ref[...]
    act8 = jnp.broadcast_to(act, (8, tok)).astype(F32).astype(BF)
    before = onehot(iota((tok, tok), 0) < iota((tok, tok), 1))
    rank = mm(act8, before)[0:1, :]
    pick = onehot((iota((CAP, tok), 0).astype(F32) == rank) & (act > 0))
    total = jnp.sum(act.astype(F32), axis=1, keepdims=True)
    cnt[x, y, z] = jnp.where(iota((1, HD), 1) == me, total, 0.0)
    loads[1].wait()
    own = mm(pick, q_ref[...]).astype(BF)
    for i in range(NA + NB):
        qa[i, x, y, z] = own[0:16, i * HD : (i + 1) * HD]
        qb[i, y, x, z] = own[16:32, i * HD : (i + 1) * HD]
    loads[2].wait()

    pl.semaphore_wait(barrier, len(peers))

    cz = copies(lambda d: (cnt.at[x, y, z],) * 2, zp, Z)
    az = copies(lambda d: (qa.at[:, x, y, z],) * 2, zp, Z)
    bz = copies(lambda d: (qb.at[:, y, x, z],) * 2, zp, Z)
    start(cz)
    start(az)
    start(bz)
    w0 = pl.ds(0, half)
    w1 = pl.ds(half, feat - half)
    wx0 = copies(lambda d: (wt.at[y, x, :, w0],) * 2, xp, X)
    wy1 = copies(lambda d: (wt.at[y, x, :, w1],) * 2, yp, Y)
    start(wx0)
    start(wy1)

    expand[...] = mm_nt(onehot(iota((tok, tok), 0) == iota((tok, tok), 1)), pick).astype(BF)
    lane, col = iota((HD, half), 0), iota((HD, half), 1)
    sel[...] = onehot(((lane & 7) == (col >> log2(HD))) & (lane < 24))
    ht[...] = jnp.zeros_like(ht)

    groups = [pl.ds(0, NA), pl.ds(NA, NB)]
    cy = copies(lambda d: (cnt.at[x, y],) * 2, yp, Y)
    ay = [copies(lambda d: (qa.at[g, x, y],) * 2, yp, Y) for g in groups]
    bx = [copies(lambda d: (qb.at[g, y, x],) * 2, xp, X) for g in groups]
    cx = copies(lambda d: (cnt.at[x],) * 2, xp, X)
    ax = [ring(lambda i, lo, hi: qa.at[g, i, :, pl.ds(lo, hi - lo)], xp, X, x) for g in groups]
    by = [ring(lambda i, lo, hi: qb.at[g, i, :, pl.ds(lo, hi - lo)], yp, Y, y) for g in groups]
    arrive(cz)
    start(cy)
    arrive(az)
    start(ay[0])
    arrive(bz)
    start(bx[0])
    start(ay[1])
    start(bx[1])
    loads[4].wait()
    for i in range(NA + NB):
        vx[i, :, :HD] = v_ref[:, i * HD : (i + 1) * HD]
        vx[i, :, HD:] = jnp.ones((tok, HD), BF)
    loads[3].wait()
    arrive(cy)
    start(cx)
    arrive(ay[0])
    start(ax[0][0])
    arrive(bx[0])
    start(by[0][0])
    arrive(ay[1])
    start(ax[1][0])
    arrive(bx[1])
    start(by[1][0])
    arrive(cx)

    counts = jnp.sum(cnt[...].reshape(X * Y * Z, HD), axis=0, keepdims=True)
    cnt8 = jnp.broadcast_to(counts, (8, HD)).astype(BF)
    size = X * Y * Z * 16

    def positions(part):
        j = iota((HD, size), 1)
        zz = (j >> 4) & (Z - 1)
        i = j >> (4 + log2(Z))
        if part == 0:
            s = ((i & (Y - 1)) * X + (i >> log2(Y))) * Z + zz
        else:
            s = j >> 4
        b = iota((HD, size), 0)
        off = mm(cnt8, onehot(b < s))[0:1, :]
        n = mm(cnt8, onehot(b == s))[0:1, :]
        r = ((j[0:1, :] & 15) + 16 * part).astype(F32)
        return jnp.where(r < n, off + r, -1.0)

    pos_a, pos_b = positions(0), positions(1)

    @pl.loop(0, Y)
    def _(yb):
        i = (iota((X * CR, size), 0) + yb * (X * CR)).astype(F32)
        pma[yb] = onehot(i == pos_a)
        pmb[yb] = onehot(i == pos_b)

    slot, b = iota((Z * CAP, HD), 0), iota((Z * CAP, HD), 1)
    off = mm_nt(onehot(b < (y * X + x) * Z + (slot >> log2(CAP))), cnt8)[:, 0:1]
    want = off + (slot[:, 0:1] & (CAP - 1)).astype(F32)
    rsel[...] = onehot(iota((Z * CAP, nr), 1).astype(F32) == want)

    scale = 1.0 / (HD**0.5 * math.log(2.0))

    def attend(first, heads, dest):
        @pl.loop(0, Y)
        def _(yb):
            lane = iota((X * CR, HD), 1)
            tile = jnp.zeros((X * CR, HD), F32)
            for i in range(heads):
                c = slice((first + i) * HD, (first + i + 1) * HD)
                rows = mm(pma[yb], qa[first + i].reshape(size, HD)) + mm(pmb[yb], qb[first + i].reshape(size, HD))
                score = mm_nt(rows.astype(BF), k_ref[:, c]) * scale
                peak = jnp.max(score, axis=1, keepdims=True)
                expo = lax.exp2(score - peak).astype(BF)
                both = mm(expo, vx[first + i])
                total = both[:, HD:]
                dest[yb, :, :, i * HD : (i + 1) * HD] = (both[:, :HD] / total).astype(BF).reshape(X, CR, HD)
                tile = jnp.where((lane & 7) == i, peak + log2_of(total), tile)
            dest[yb, :, :, heads * HD :] = pack_stat(tile).reshape(X, CR, HD)

    arrive(ax[0][0])
    start(ax[0][1])
    arrive(by[0][0])
    start(by[0][1])
    arrive(ax[0][1])
    arrive(by[0][1])
    attend(0, NA, pa)
    sa = copies(lambda d: (pa.at[(y + d) & (Y - 1)], ra.at[d - 1]), yp, Y)
    start(sa)
    arrive(ax[1][0])
    start(ax[1][1])
    arrive(by[1][0])
    start(by[1][1])
    arrive(ax[1][1])
    arrive(by[1][1])
    attend(NA, NB, pb)
    sb = copies(lambda d: (pb.at[:, (x + d) & (X - 1)], rb.at[d - 1]), xp, X)
    start(sb)

    arrive(wx0)
    arrive(wy1)
    wy0 = copies(lambda d: (wt.at[y, :, :, w0],) * 2, yp, Y)
    wx1 = copies(lambda d: (wt.at[:, x, :, w1],) * 2, xp, X)
    arrive(sa)

    @pl.loop(0, X)
    def _(i):
        mean, logs = merge([pa[y, i]] + [ra[d, i] for d in range(Y - 1)], NA, sel[...])
        a2[i, :, :half] = mean.astype(BF)
        a2[i, :, half:] = stat_of(logs, NA)

    sa2 = copies(lambda d: (a2.at[(x + d) & (X - 1)], ra2.at[d - 1]), xp, X)
    start(sa2)
    start(wy0)
    arrive(sb)

    @pl.loop(0, Y)
    def _(i):
        mean, logs = merge([pb[i, x]] + [rb[d, i] for d in range(X - 1)], NB, sel[...])
        b2[i, :, : NB * HD] = mean.astype(BF)
        b2[i, :, NB * HD :] = stat_of(logs, NB)

    sb2 = copies(lambda d: (b2.at[(y + d) & (Y - 1)], rb2.at[d - 1]), yp, Y)
    start(sb2)
    start(wx1)
    arrive(sa2)
    mean, logs = merge([a2[x]] + [ra2[d] for d in range(X - 1)], NA, sel[...])
    a3[:, :half] = mean.astype(BF)
    a3[:, half:] = stat_of(logs, NA)
    sa3 = copies(lambda d: (a3, ra3.at[d - 1]), zp, Z)
    start(sa3)
    arrive(sb2)
    mean, logs = merge([b2[y]] + [rb2[d] for d in range(Y - 1)], NB, sel[...])
    b3[:, : NB * HD] = mean.astype(BF)
    b3[:, NB * HD :] = stat_of(logs, NB)
    sb3 = copies(lambda d: (b3, rb3.at[d - 1]), zp, Z)
    start(sb3)
    arrive(sa3)
    attn_a = merge([a3[...]] + [ra3[d] for d in range(Z - 1)], NA, sel[...])[0].astype(BF)
    arrive(wy0)
    arrive(wx1)
    arrive(sb3)
    attn_b = merge([b3[...]] + [rb3[d] for d in range(Z - 1)], NB, sel[...])[0].astype(BF)

    pieces = X * Y // H
    for o in range(H):
        yy, xx = o * pieces // X, o * pieces % X
        w_o = wt[yy, xx : xx + pieces].reshape(pieces * wc, feat)
        term = mm_nt(attn_a, w_o[:, :half]) + mm_nt(attn_b, w_o[:, half:])
        ht[o, :, : pieces * wc] = term.astype(BF)
    sh = copies(lambda d: (ht.at[(h + d) & (H - 1)], hr.at[d - 1]), hp, H)
    start(sh)
    proj = ht[h].astype(F32)
    for d in range(1, H):
        arrive(sh[d - 1 : d])
        proj = proj + hr[d - 1].astype(F32)
    fin[y, x] = proj.astype(BF)

    f0, f1 = pl.ds(0, HD), pl.ds(HD, HD)
    fx0 = copies(lambda d: (fin.at[y, x, :, f0],) * 2, xp, X)
    fy1 = copies(lambda d: (fin.at[y, x, :, f1],) * 2, yp, Y)
    start(fx0)
    start(fy1)
    fy0 = copies(lambda d: (fin.at[y, :, :, f0],) * 2, yp, Y)
    fx1 = copies(lambda d: (fin.at[:, x, :, f1],) * 2, xp, X)
    arrive(fx0)
    start(fy0)
    arrive(fy1)
    start(fx1)
    arrive(fy0)
    arrive(fx1)
    zs[...] = mm(rsel[...], fin[...].reshape(nr, 2 * HD)).astype(BF).reshape(Z, CAP, 2 * HD)
    sz = copies(lambda d: (zs.at[(z + d) & (Z - 1)], zr.at[d - 1]), zp, Z)
    start(sz)

    def place(rows, zz):
        l, c = iota((2 * HD, feat), 0), iota((2 * HD, feat), 1)
        second = l >= wc
        at = jnp.where(second, Z * wc - wc, 0) + zz * wc + l
        return mm(rows, onehot((c == at) & (l < pieces * wc)))

    rows = place(zs[z], z)
    for d in range(1, Z):
        arrive(sz[d - 1 : d])
        rows = rows + place(zr[d - 1], (z - d) & (Z - 1))
    loads[5].wait()
    loads[6].wait()
    grown = mm(expand[...], rows.astype(BF))
    live = mm(expand[...], jnp.ones((CAP, feat), BF)) > 0.5
    out_ref[...] = jnp.where(live, hid_ref[...].astype(F32) + grown, cac_ref[...].astype(F32)).astype(BF)
    for c in every:
        c.wait_send()


def shards(queries, keys, values, hidden, cached, active, w_out):
    tok, feat = queries.shape
    wc = w_out.shape[1]
    size = X * Y * Z * 16
    wa, wb = (NA + 1) * HD, (NB + 1) * HD
    n_copies = 160
    vmem = pltpu.VMEM
    scratch = [
        vmem((tok, feat), BF),
        vmem((tok, feat), BF),
        vmem((tok, feat), BF),
        vmem((tok, feat), BF),
        vmem((tok, feat), BF),
        vmem((1, tok), jnp.int32),
        vmem((NA + NB, X, Y, Z, 16, HD), BF),
        vmem((NA + NB, Y, X, Z, 16, HD), BF),
        vmem((X, Y, Z, 1, HD), F32),
        vmem((Y, X, wc, feat), BF),
        vmem((Y, X * CR, size), BF),
        vmem((Y, X * CR, size), BF),
        vmem((NA + NB, tok, 2 * HD), BF),
        vmem((HD, NA * HD), BF),
        vmem((Z * CAP, Y * X * CR), BF),
        vmem((tok, CAP), BF),
        vmem((Y, X, CR, wa), BF),
        vmem((Y, X, CR, wb), BF),
        vmem((max(Y - 1, 1), X, CR, wa), BF),
        vmem((max(X - 1, 1), Y, CR, wb), BF),
        vmem((X, CR, wa), BF),
        vmem((Y, CR, wb), BF),
        vmem((max(X - 1, 1), CR, wa), BF),
        vmem((max(Y - 1, 1), CR, wb), BF),
        vmem((CR, wa), BF),
        vmem((CR, wb), BF),
        vmem((Z - 1, CR, wa), BF),
        vmem((Z - 1, CR, wb), BF),
        vmem((H, CR, 2 * HD), BF),
        vmem((H - 1, CR, 2 * HD), BF),
        vmem((Y, X, CR, 2 * HD), BF),
        vmem((Z, CAP, 2 * HD), BF),
        vmem((Z - 1, CAP, 2 * HD), BF),
        pltpu.SemaphoreType.DMA((n_copies,)),
        pltpu.SemaphoreType.DMA((n_copies,)),
        pltpu.SemaphoreType.DMA((7,)),
    ]
    return pl.pallas_call(
        body,
        out_shape=jax.ShapeDtypeStruct((tok, feat), BF),
        in_specs=[pl.BlockSpec(memory_space=pl.ANY)] * 7,
        out_specs=pl.BlockSpec(memory_space=pltpu.VMEM),
        scratch_shapes=scratch,
        compiler_params=pltpu.CompilerParams(
            collective_id=0, has_side_effects=True, vmem_limit_bytes=60 * 2**20
        ),
    )(queries, keys, values, hidden, cached, active.reshape(1, tok), w_out.T)


def solution(mesh):
    placed = (
        P("seq", "head"),
        P("seq", "head"),
        P("seq", "head"),
        P("seq", "head"),
        P("seq", "head"),
        P("seq"),
        P("head", "seq"),
    )
    return jax.shard_map(
        shards, mesh=mesh, in_specs=placed, out_specs=P("seq", "head"), check_vma=False
    )
```

```python
import math

import jax
import jax.numpy as jnp
from jax import lax
from jax.experimental import pallas as pl
from jax.experimental.pallas import tpu as pltpu
from jax.sharding import PartitionSpec as P

X, Y, Z, H = 4, 4, 4, 8
HD = 128
CAP = 32
BF = jnp.bfloat16
F32 = jnp.float32
NA, NB = 3, 2
MESH = pl.DeviceIdType.MESH


def log2(n):
    return n.bit_length() - 1


def iota(shape, dim):
    return lax.broadcasted_iota(jnp.int32, shape, dim)


def onehot(cond):
    return jnp.where(cond, 1.0, 0.0).astype(BF)


def log2_of(v):
    return jnp.log(v) * (1.0 / math.log(2.0))


def mm(a, b):
    return jnp.dot(a, b, preferred_element_type=F32)


def mm_nt(a, b):
    return lax.dot_general(a, b, (((1,), (1,)), ((), ())), preferred_element_type=F32)


def pack_stat(tile):
    lane = iota(tile.shape, 1)
    hi = tile.astype(BF).astype(F32)
    rest = tile - hi
    mid = rest.astype(BF).astype(F32)
    low = rest - mid
    return jnp.where(lane < 8, hi, jnp.where(lane < 16, mid, jnp.where(lane < 24, low, 0.0))).astype(BF)


def merge(sources, heads, sel):
    width = heads * HD
    logs = [mm(s[:, width:], sel[:, :width]) for s in sources]
    top = logs[0]
    for part in logs[1:]:
        top = jnp.maximum(top, part)
    total, mixed = None, None
    for s, part in zip(sources, logs):
        w = lax.exp2(part - top)
        term = w * s[:, :width].astype(F32)
        total = w if total is None else total + w
        mixed = term if mixed is None else mixed + term
    return mixed / total, top + log2_of(total)


def stat_of(logs, heads):
    lane = iota((logs.shape[0], HD), 1)
    tile = jnp.zeros((logs.shape[0], HD), F32)
    for h in range(heads):
        tile = jnp.where((lane & 7) == h, logs[:, h * HD : (h + 1) * HD], tile)
    return pack_stat(tile)


def body(
    q_hbm, k_hbm, v_hbm, hid_hbm, cac_hbm, act_hbm, w_hbm, out_ref,
    q_ref, hid_ref, cac_ref, act_ref,
    ka, va, kb, vb, qa, qb, wt, sel, expand,
    sum_a, peak_a, sum_b, peak_b,
    pa, pb, ra, rb, a2, b2, ra2, rb2, at,
    ht, hr, zs, zr, send_sem, recv_sem, load_sem,
):
    tok, feat = q_ref.shape
    wc = w_hbm.shape[0]
    half = NA * HD
    me, h = lax.axis_index("seq"), lax.axis_index("head")
    z = me & (Z - 1)
    x = (me >> log2(Z)) & (X - 1)
    y = me >> log2(Z * X)

    def xp(d):
        return (y * X + ((x + d) & (X - 1))) * Z + z, h

    def yp(d):
        return (((y + d) & (Y - 1)) * X + x) * Z + z, h

    def zp(d):
        return (y * X + x) * Z + ((z + d) & (Z - 1)), h

    def hp(d):
        return me, (h + d) & (H - 1)

    barrier = pltpu.get_barrier_semaphore()
    peers = (
        [xp(d) for d in range(1, X)] + [yp(d) for d in range(1, Y)] + [zp(d) for d in range(1, Z)] + [hp(d) for d in range(1, H)]
    )
    for p in peers:
        pl.semaphore_signal(barrier, inc=1, device_id=p, device_id_type=MESH)

    lo, hi = pl.ds(0, half), pl.ds(half, feat - half)
    loads = [
        pltpu.make_async_copy(src, dst, load_sem.at[i])
        for i, (src, dst) in enumerate(
            [
                (act_hbm, act_ref), (q_hbm, q_ref),
                (k_hbm.at[:, lo], ka.at[x]), (k_hbm.at[:, hi], kb.at[y]),
                (v_hbm.at[:, lo], va.at[x]), (v_hbm.at[:, hi], vb.at[y]),
                (w_hbm, wt.at[y, x]), (hid_hbm, hid_ref), (cac_hbm, cac_ref),
            ]
        )
    ]
    for c in loads:
        c.start()

    counter = [0]
    every = []

    def copies(make, peer, steps):
        found = []
        for d in steps:
            i = counter[0]
            counter[0] += 1
            src, dst = make(d)
            found.append(
                pltpu.make_async_remote_copy(
                    src_ref=src, dst_ref=dst, send_sem=send_sem.at[i], recv_sem=recv_sem.at[i],
                    device_id=peer(d), device_id_type=MESH,
                )
            )
        return found

    def start(cs):
        for c in cs:
            c.start()
        every.extend(cs)

    def arrive(cs):
        for c in cs:
            c.wait_recv()

    def near(n):
        return [1, n - 1] if n > 2 else list(range(1, n))

    def far(n):
        return list(range(2, n - 1))

    every_x, every_y, every_z, every_h = range(1, X), range(1, Y), range(1, Z), range(1, H)

    loads[0].wait()
    act = act_ref[...]
    act8 = jnp.broadcast_to(act, (8, tok)).astype(F32).astype(BF)
    before = onehot(iota((tok, tok), 0) < iota((tok, tok), 1))
    rank = mm(act8, before)[0:1, :]
    pick = onehot((iota((CAP, tok), 0).astype(F32) == rank) & (act > 0))
    loads[1].wait()
    own = mm(pick, q_ref[...]).astype(BF)
    qa[y, z] = own[:, :half]
    qb[x, z] = own[:, half:]
    for c in loads[2:7]:
        c.wait()

    pl.semaphore_wait(barrier, len(peers))

    az = copies(lambda d: (qa.at[y, z],) * 2, zp, every_z)
    bz = copies(lambda d: (qb.at[x, z],) * 2, zp, every_z)
    start(az)
    start(bz)
    ka1 = copies(lambda d: (ka.at[x],) * 2, xp, near(X)) + copies(lambda d: (va.at[x],) * 2, xp, near(X))
    kb1 = copies(lambda d: (kb.at[y],) * 2, yp, near(Y)) + copies(lambda d: (vb.at[y],) * 2, yp, near(Y))
    ka2 = copies(lambda d: (ka.at[x],) * 2, xp, far(X)) + copies(lambda d: (va.at[x],) * 2, xp, far(X))
    kb2 = copies(lambda d: (kb.at[y],) * 2, yp, far(Y)) + copies(lambda d: (vb.at[y],) * 2, yp, far(Y))
    start(ka1)
    start(kb1)

    expand[...] = mm_nt(onehot(iota((tok, tok), 0) == iota((tok, tok), 1)), pick).astype(BF)
    lane, col = iota((HD, half), 0), iota((HD, half), 1)
    sel[...] = onehot(((lane & 7) == (col >> log2(HD))) & (lane < 24))

    ay = copies(lambda d: (qa.at[y],) * 2, yp, every_y)
    bx = copies(lambda d: (qb.at[x],) * 2, xp, every_x)
    arrive(az)
    start(ay)
    arrive(bz)
    start(bx)
    start(ka2)
    start(kb2)

    wx0 = copies(lambda d: (wt.at[y, x, :, lo],) * 2, xp, every_x)
    wy1 = copies(lambda d: (wt.at[y, x, :, hi],) * 2, yp, every_y)
    wy0 = copies(lambda d: (wt.at[y, :, :, lo],) * 2, yp, every_y)
    wx1 = copies(lambda d: (wt.at[:, x, :, hi],) * 2, xp, every_x)
    start(wx0)
    start(wy1)

    scale = 1.0 / (HD**0.5 * math.log(2.0))
    ones = jnp.ones((tok, HD), BF)
    group = Z * CAP

    def attend(heads, rows, k, v, blocks, sums, peaks, dest, first, last):
        @pl.loop(0, rows.shape[0])
        def _(g):
            lane = iota((group, HD), 1)
            tile = jnp.zeros((group, HD), F32)
            for i in range(heads):
                c = slice(i * HD, (i + 1) * HD)
                query = rows[g, :, :, c].reshape(group, HD)
                scores = [mm_nt(query, k[b, :, c]) * scale for b in blocks]
                peak = jnp.max(scores[0], axis=1, keepdims=True)
                for score in scores[1:]:
                    peak = jnp.maximum(peak, jnp.max(score, axis=1, keepdims=True))
                if not first:
                    old = peaks[g, i]
                    peak = jnp.maximum(old, peak)
                both = None
                for b, score in zip(blocks, scores):
                    expo = lax.exp2(score - peak[:, 0:1]).astype(BF)
                    part = mm(expo, jnp.concatenate([v[b, :, c], ones], axis=1))
                    both = part if both is None else both + part
                if not first:
                    fade = lax.exp2(old - peak)
                    both = both + sums[g, i] * jnp.concatenate([fade, fade], axis=1)
                if last:
                    total = both[:, HD:]
                    dest[g, :, :, c] = (both[:, :HD] / total).astype(BF).reshape(Z, CAP, HD)
                    tile = jnp.where((lane & 7) == i, peak + log2_of(total), tile)
                else:
                    sums[g, i] = both
                    peaks[g, i] = jnp.broadcast_to(peak, (group, HD))
            if last:
                dest[g, :, :, heads * HD :] = pack_stat(tile).reshape(Z, CAP, HD)

    def near_blocks(at_, n):
        return [at_] + [(at_ - d) & (n - 1) for d in near(n)]

    def far_blocks(at_, n):
        return [(at_ - d) & (n - 1) for d in far(n)]

    arrive(ay)
    arrive(ka1)
    attend(NA, qa, ka, va, near_blocks(x, X), sum_a, peak_a, pa, True, X <= 3)
    arrive(bx)
    arrive(kb1)
    attend(NB, qb, kb, vb, near_blocks(y, Y), sum_b, peak_b, pb, True, Y <= 3)
    arrive(ka2)
    if X > 3:
        attend(NA, qa, ka, va, far_blocks(x, X), sum_a, peak_a, pa, False, True)
    sa = copies(lambda d: (pa.at[(y + d) & (Y - 1)], ra.at[d - 1]), yp, every_y)
    start(sa)
    arrive(kb2)
    if Y > 3:
        attend(NB, qb, kb, vb, far_blocks(y, Y), sum_b, peak_b, pb, False, True)
    sb = copies(lambda d: (pb.at[(x + d) & (X - 1)], rb.at[d - 1]), xp, every_x)
    start(sb)
    arrive(wx0)
    arrive(wy1)
    start(wy0)
    start(wx1)

    arrive(sa)

    @pl.loop(0, Z)
    def _(i):
        mean, logs = merge([pa[y, i]] + [ra[d, i] for d in range(Y - 1)], NA, sel[...])
        a2[i, :, :half] = mean.astype(BF)
        a2[i, :, half:] = stat_of(logs, NA)

    sa2 = copies(lambda d: (a2.at[(z + d) & (Z - 1)], ra2.at[d - 1]), zp, every_z)
    start(sa2)
    arrive(sb)

    @pl.loop(0, Z)
    def _(i):
        mean, logs = merge([pb[x, i]] + [rb[d, i] for d in range(X - 1)], NB, sel[...])
        b2[i, :, : NB * HD] = mean.astype(BF)
        b2[i, :, NB * HD :] = stat_of(logs, NB)

    sb2 = copies(lambda d: (b2.at[(z + d) & (Z - 1)], rb2.at[d - 1]), zp, every_z)
    start(sb2)
    arrive(sa2)
    at[z, :, :half] = merge([a2[z]] + [ra2[d] for d in range(Z - 1)], NA, sel[...])[0].astype(BF)
    arrive(sb2)
    at[z, :, half:] = merge([b2[z]] + [rb2[d] for d in range(Z - 1)], NB, sel[...])[0].astype(BF)
    tz = copies(lambda d: (at.at[z],) * 2, zp, every_z)
    start(tz)
    arrive(tz)
    arrive(wy0)
    arrive(wx1)

    pieces = X * Y // H
    extra = pieces * wc - HD
    attn = at[...].reshape(group, feat)
    for o in range(H):
        yy, xx = o * pieces // X, o * pieces % X
        term = mm_nt(attn, wt[yy, xx : xx + pieces].reshape(pieces * wc, feat))
        ht[o, 0:group] = term[:, :HD].astype(BF)
        for i in range(Z):
            ht[o, group:, i * extra : (i + 1) * extra] = term[i * CAP : (i + 1) * CAP, HD:].astype(BF)
    sh = copies(lambda d: (ht.at[(h + d) & (H - 1)], hr.at[d - 1]), hp, every_h)
    start(sh)
    proj = ht[h].astype(F32)
    for d in every_h:
        arrive(sh[d - 1 : d])
        proj = proj + hr[d - 1].astype(F32)
    lane = iota((CAP, HD), 1)
    for i in range(Z):
        zs[i, 0:CAP] = proj[i * CAP : (i + 1) * CAP].astype(BF)
        zs[i, CAP:] = jnp.where((lane >= i * extra) & (lane < (i + 1) * extra), proj[group:], 0.0).astype(BF)

    sz = copies(lambda d: (zs.at[(z + d) & (Z - 1)], zr.at[d - 1]), zp, every_z)
    start(sz)

    def place(rows, zz):
        l, c = iota((HD, feat), 0), iota((HD, feat), 1)
        p1 = l
        p2 = HD + l - z * extra
        t1 = jnp.where(p1 >= wc, (Z - 1) * wc, 0) + zz * wc + p1
        t2 = jnp.where(p2 >= wc, (Z - 1) * wc, 0) + zz * wc + p2
        inside = (l >= z * extra) & (l < (z + 1) * extra)
        return mm(rows[0:CAP], onehot(c == t1)) + mm(rows[CAP:], onehot((c == t2) & inside))

    rows = place(zs[z], z)
    for d in every_z:
        arrive(sz[d - 1 : d])
        rows = rows + place(zr[d - 1], (z - d) & (Z - 1))
    loads[7].wait()
    loads[8].wait()
    grown = mm(expand[...], rows.astype(BF))
    live = mm(expand[...], jnp.ones((CAP, feat), BF)) > 0.5
    out_ref[...] = jnp.where(live, hid_ref[...].astype(F32) + grown, cac_ref[...].astype(F32)).astype(BF)
    for c in every:
        c.wait_send()


def shards(queries, keys, values, hidden, cached, active, w_out):
    tok, feat = queries.shape
    wc = w_out.shape[1]
    fa, fb = NA * HD, NB * HD
    wa, wb = fa + HD, fb + HD
    group = Z * CAP
    n_copies = 120
    vmem = pltpu.VMEM
    scratch = [
        vmem((tok, feat), BF),
        vmem((tok, feat), BF),
        vmem((tok, feat), BF),
        vmem((1, tok), jnp.int32),
        vmem((X, tok, fa), BF),
        vmem((X, tok, fa), BF),
        vmem((Y, tok, fb), BF),
        vmem((Y, tok, fb), BF),
        vmem((Y, Z, CAP, fa), BF),
        vmem((X, Z, CAP, fb), BF),
        vmem((Y, X, wc, feat), BF),
        vmem((HD, fa), BF),
        vmem((tok, CAP), BF),
        vmem((Y, NA, group, 2 * HD), F32),
        vmem((Y, NA, group, HD), F32),
        vmem((X, NB, group, 2 * HD), F32),
        vmem((X, NB, group, HD), F32),
        vmem((Y, Z, CAP, wa), BF),
        vmem((X, Z, CAP, wb), BF),
        vmem((max(Y - 1, 1), Z, CAP, wa), BF),
        vmem((max(X - 1, 1), Z, CAP, wb), BF),
        vmem((Z, CAP, wa), BF),
        vmem((Z, CAP, wb), BF),
        vmem((Z - 1, CAP, wa), BF),
        vmem((Z - 1, CAP, wb), BF),
        vmem((Z, CAP, feat), BF),
        vmem((H, group + CAP, HD), BF),
        vmem((H - 1, group + CAP, HD), BF),
        vmem((Z, 2 * CAP, HD), BF),
        vmem((Z - 1, 2 * CAP, HD), BF),
        pltpu.SemaphoreType.DMA((n_copies,)),
        pltpu.SemaphoreType.DMA((n_copies,)),
        pltpu.SemaphoreType.DMA((9,)),
    ]
    return pl.pallas_call(
        body,
        out_shape=jax.ShapeDtypeStruct((tok, feat), BF),
        in_specs=[pl.BlockSpec(memory_space=pl.ANY)] * 7,
        out_specs=pl.BlockSpec(memory_space=pltpu.VMEM),
        scratch_shapes=scratch,
        compiler_params=pltpu.CompilerParams(
            collective_id=0, has_side_effects=True, vmem_limit_bytes=60 * 2**20
        ),
    )(queries, keys, values, hidden, cached, active.reshape(1, tok), w_out.T)


def solution(mesh):
    placed = (
        P("seq", "head"),
        P("seq", "head"),
        P("seq", "head"),
        P("seq", "head"),
        P("seq", "head"),
        P("seq"),
        P("head", "seq"),
    )
    return jax.shard_map(
        shards, mesh=mesh, in_specs=placed, out_specs=P("seq", "head"), check_vma=False
    )
```

```python
import math

import jax
import jax.numpy as jnp
from jax import lax
from jax.experimental import pallas as pl
from jax.experimental.pallas import tpu as pltpu
from jax.sharding import PartitionSpec as P

X, Y, Z, H = 4, 4, 4, 8
HD = 128
CAP = 32
BF = jnp.bfloat16
F32 = jnp.float32
NA, NB = 3, 2
MESH = pl.DeviceIdType.MESH


def log2(n):
    return n.bit_length() - 1


def iota(shape, dim):
    return lax.broadcasted_iota(jnp.int32, shape, dim)


def onehot(cond):
    return jnp.where(cond, 1.0, 0.0).astype(BF)


def log2_of(v):
    return jnp.log(v) * (1.0 / math.log(2.0))


def mm(a, b):
    return jnp.dot(a, b, preferred_element_type=F32)


def mm_nt(a, b):
    return lax.dot_general(a, b, (((1,), (1,)), ((), ())), preferred_element_type=F32)


def pack_stat(tile):
    lane = iota(tile.shape, 1)
    hi = tile.astype(BF).astype(F32)
    rest = tile - hi
    mid = rest.astype(BF).astype(F32)
    low = rest - mid
    return jnp.where(lane < 8, hi, jnp.where(lane < 16, mid, jnp.where(lane < 24, low, 0.0))).astype(BF)


def merge(sources, heads, sel):
    width = heads * HD
    logs = [mm(s[:, width:], sel[:, :width]) for s in sources]
    top = logs[0]
    for part in logs[1:]:
        top = jnp.maximum(top, part)
    total, mixed = None, None
    for s, part in zip(sources, logs):
        w = lax.exp2(part - top)
        term = w * s[:, :width].astype(F32)
        total = w if total is None else total + w
        mixed = term if mixed is None else mixed + term
    return mixed / total, top + log2_of(total)


def stat_of(logs, heads):
    lane = iota((logs.shape[0], HD), 1)
    tile = jnp.zeros((logs.shape[0], HD), F32)
    for h in range(heads):
        tile = jnp.where((lane & 7) == h, logs[:, h * HD : (h + 1) * HD], tile)
    return pack_stat(tile)


def body(
    q_hbm, k_hbm, v_hbm, hid_hbm, cac_hbm, act_hbm, w_hbm, out_ref,
    q_ref, hid_ref, cac_ref, act_ref,
    ka, va, kb, vb, qa, qb, wt, sel, expand,
    sum_a, peak_a, sum_b, peak_b,
    pa, pb, ra, rb, a2, b2, ra2, rb2, at,
    ht, hc, hs, hr, zs, zr, send_sem, recv_sem, load_sem,
):
    tok, feat = q_ref.shape
    wc = w_hbm.shape[0]
    half = NA * HD
    me, h = lax.axis_index("seq"), lax.axis_index("head")
    z = me & (Z - 1)
    x = (me >> log2(Z)) & (X - 1)
    y = me >> log2(Z * X)

    def xp(d):
        return (y * X + ((x + d) & (X - 1))) * Z + z, h

    def yp(d):
        return (((y + d) & (Y - 1)) * X + x) * Z + z, h

    def zp(d):
        return (y * X + x) * Z + ((z + d) & (Z - 1)), h

    def cp(d):
        return me, h ^ 1

    def hp(d):
        return me, (((h >> 1) + d) & (H // 2 - 1)) * 2 + (h & 1)

    barrier = pltpu.get_barrier_semaphore()
    peers = (
        [xp(d) for d in range(1, X)] + [yp(d) for d in range(1, Y)] + [zp(d) for d in range(1, Z)] + [hp(d) for d in range(1, H // 2)] + [cp(1)]
    )
    for p in peers:
        pl.semaphore_signal(barrier, inc=1, device_id=p, device_id_type=MESH)

    lo, hi = pl.ds(0, half), pl.ds(half, feat - half)
    loads = [
        pltpu.make_async_copy(src, dst, load_sem.at[i])
        for i, (src, dst) in enumerate(
            [
                (act_hbm, act_ref), (q_hbm, q_ref),
                (k_hbm.at[:, lo], ka.at[x]), (k_hbm.at[:, hi], kb.at[y]),
                (v_hbm.at[:, lo], va.at[x]), (v_hbm.at[:, hi], vb.at[y]),
                (w_hbm, wt.at[y, x]), (hid_hbm, hid_ref), (cac_hbm, cac_ref),
            ]
        )
    ]
    for c in loads:
        c.start()

    counter = [0]
    every = []

    def copies(make, peer, steps):
        found = []
        for d in steps:
            i = counter[0]
            counter[0] += 1
            src, dst = make(d)
            found.append(
                pltpu.make_async_remote_copy(
                    src_ref=src, dst_ref=dst, send_sem=send_sem.at[i], recv_sem=recv_sem.at[i],
                    device_id=peer(d), device_id_type=MESH,
                )
            )
        return found

    def start(cs):
        for c in cs:
            c.start()
        every.extend(cs)

    def arrive(cs):
        for c in cs:
            c.wait_recv()

    def near(n):
        return [1, n - 1] if n > 2 else list(range(1, n))

    def far(n):
        return list(range(2, n - 1))

    def relay(block, peer, n, at_):
        if n <= 3:
            return []
        on = copies(lambda d: (block((at_ - 1) & (n - 1), 0),) * 2, peer, [1])
        return on + copies(lambda d: (block((at_ + 1) & (n - 1), 1),) * 2, peer, [n - 1])

    every_x, every_y, every_z, every_h = range(1, X), range(1, Y), range(1, Z), range(1, H // 2)

    pl.semaphore_wait(barrier, len(peers))

    ka1 = copies(lambda d: (k_hbm.at[:, lo], ka.at[x]), xp, near(X))
    va1 = copies(lambda d: (v_hbm.at[:, lo], va.at[x]), xp, near(X))
    kb1 = copies(lambda d: (k_hbm.at[:, hi], kb.at[y]), yp, near(Y))
    vb1 = copies(lambda d: (v_hbm.at[:, hi], vb.at[y]), yp, near(Y))
    start(ka1)
    start(kb1)
    start(va1)
    start(vb1)

    loads[0].wait()
    act = act_ref[...]
    act8 = jnp.broadcast_to(act, (8, tok)).astype(F32).astype(BF)
    before = onehot(iota((tok, tok), 0) < iota((tok, tok), 1))
    rank = mm(act8, before)[0:1, :]
    pick = onehot((iota((CAP, tok), 0).astype(F32) == rank) & (act > 0))
    loads[1].wait()
    own = mm(pick, q_ref[...]).astype(BF)
    qa[y, z] = own[:, :half]
    qb[x, z] = own[:, half:]
    az = copies(lambda d: (qa.at[y, z],) * 2, zp, every_z)
    bz = copies(lambda d: (qb.at[x, z],) * 2, zp, every_z)
    start(az)
    start(bz)

    expand[...] = mm_nt(onehot(iota((tok, tok), 0) == iota((tok, tok), 1)), pick).astype(BF)
    lane, col = iota((HD, half), 0), iota((HD, half), 1)
    sel[...] = onehot(((lane & 7) == (col >> log2(HD))) & (lane < 24))

    for c in loads[2:7]:
        c.wait()
    ay = copies(lambda d: (qa.at[y],) * 2, yp, every_y)
    bx = copies(lambda d: (qb.at[x],) * 2, xp, every_x)
    ka2 = relay(lambda i, part: ka.at[i, pl.ds(part * (tok // 2), tok // 2)], xp, X, x)
    va2 = relay(lambda i, part: va.at[i, pl.ds(part * (tok // 2), tok // 2)], xp, X, x)
    kb2 = relay(lambda i, part: kb.at[i, pl.ds(part * (tok // 2), tok // 2)], yp, Y, y)
    vb2 = relay(lambda i, part: vb.at[i, pl.ds(part * (tok // 2), tok // 2)], yp, Y, y)
    arrive(az)
    start(ay)
    arrive(bz)
    start(bx)
    arrive(kb1)
    start(kb2)
    arrive(ka1)
    start(ka2)
    arrive(vb1)
    start(vb2)
    arrive(va1)
    start(va2)

    cut = [pl.ds(0, 48), pl.ds(48, wc - 48)]
    wy0 = copies(lambda d: (wt.at[y, x, :, lo],) * 2, yp, every_y)
    wx1 = copies(lambda d: (wt.at[y, x, :, hi],) * 2, xp, every_x)
    wx0 = copies(lambda d: (wt.at[:, x, :, lo],) * 2, xp, near(X))
    wy1 = copies(lambda d: (wt.at[y, :, :, hi],) * 2, yp, near(Y))
    wx0 = [wx0, relay(lambda i, part: wt.at[:, i, cut[part], lo], xp, X, x)]
    wy1 = [wy1, relay(lambda i, part: wt.at[i, :, cut[part], hi], yp, Y, y)]

    scale = 1.0 / (HD**0.5 * math.log(2.0))
    ones = jnp.ones((tok, HD), BF)
    group = Z * CAP

    def attend(heads, rows, k, v, blocks, sums, peaks, dest, first, last):
        @pl.loop(0, rows.shape[0])
        def _(g):
            lane = iota((group, HD), 1)
            tile = jnp.zeros((group, HD), F32)
            for i in range(heads):
                c = slice(i * HD, (i + 1) * HD)
                query = rows[g, :, :, c].reshape(group, HD)
                scores = [mm_nt(query, k[b, :, c]) * scale for b in blocks]
                peak = jnp.max(scores[0], axis=1, keepdims=True)
                for score in scores[1:]:
                    peak = jnp.maximum(peak, jnp.max(score, axis=1, keepdims=True))
                if not first:
                    old = peaks[g, i]
                    peak = jnp.maximum(old, peak)
                both = None
                for b, score in zip(blocks, scores):
                    expo = lax.exp2(score - peak[:, 0:1]).astype(BF)
                    part = mm(expo, jnp.concatenate([v[b, :, c], ones], axis=1))
                    both = part if both is None else both + part
                if not first:
                    fade = lax.exp2(old - peak)
                    both = both + sums[g, i] * jnp.concatenate([fade, fade], axis=1)
                if last:
                    total = both[:, HD:]
                    dest[g, :, :, c] = (both[:, :HD] / total).astype(BF).reshape(Z, CAP, HD)
                    tile = jnp.where((lane & 7) == i, peak + log2_of(total), tile)
                else:
                    sums[g, i] = both
                    peaks[g, i] = jnp.broadcast_to(peak, (group, HD))
            if last:
                dest[g, :, :, heads * HD :] = pack_stat(tile).reshape(Z, CAP, HD)

    def near_blocks(at_, n):
        return [at_] + [(at_ - d) & (n - 1) for d in near(n)]

    def far_blocks(at_, n):
        return [(at_ - d) & (n - 1) for d in far(n)]

    arrive(ay)
    attend(NA, qa, ka, va, near_blocks(x, X), sum_a, peak_a, pa, True, X <= 3)
    arrive(bx)
    attend(NB, qb, kb, vb, near_blocks(y, Y), sum_b, peak_b, pb, True, Y <= 3)
    start(wy0)
    start(wx1)
    arrive(ka2)
    arrive(va2)
    if X > 3:
        attend(NA, qa, ka, va, far_blocks(x, X), sum_a, peak_a, pa, False, True)
    sa = copies(lambda d: (pa.at[(y + d) & (Y - 1)], ra.at[d - 1]), yp, every_y)
    start(sa)
    arrive(kb2)
    arrive(vb2)
    if Y > 3:
        attend(NB, qb, kb, vb, far_blocks(y, Y), sum_b, peak_b, pb, False, True)
    sb = copies(lambda d: (pb.at[(x + d) & (X - 1)], rb.at[d - 1]), xp, every_x)
    start(sb)
    arrive(wy0)
    arrive(wx1)
    start(wx0[0])
    start(wy1[0])

    arrive(sa)

    @pl.loop(0, Z)
    def _(i):
        mean, logs = merge([pa[y, i]] + [ra[d, i] for d in range(Y - 1)], NA, sel[...])
        a2[i, :, :half] = mean.astype(BF)
        a2[i, :, half:] = stat_of(logs, NA)

    sa2 = copies(lambda d: (a2.at[(z + d) & (Z - 1)], ra2.at[d - 1]), zp, every_z)
    start(sa2)
    arrive(sb)

    @pl.loop(0, Z)
    def _(i):
        mean, logs = merge([pb[x, i]] + [rb[d, i] for d in range(X - 1)], NB, sel[...])
        b2[i, :, : NB * HD] = mean.astype(BF)
        b2[i, :, NB * HD :] = stat_of(logs, NB)

    sb2 = copies(lambda d: (b2.at[(z + d) & (Z - 1)], rb2.at[d - 1]), zp, every_z)
    start(sb2)
    arrive(wx0[0])
    start(wx0[1])
    arrive(wy1[0])
    start(wy1[1])
    arrive(sa2)
    at[z, :, :half] = merge([a2[z]] + [ra2[d] for d in range(Z - 1)], NA, sel[...])[0].astype(BF)
    arrive(sb2)
    at[z, :, half:] = merge([b2[z]] + [rb2[d] for d in range(Z - 1)], NB, sel[...])[0].astype(BF)
    tz = copies(lambda d: (at.at[z],) * 2, zp, every_z)
    start(tz)
    arrive(tz)
    arrive(wx0[1])
    arrive(wy1[1])

    pieces = X * Y // H
    extra = pieces * wc - HD
    attn = at[...].reshape(group, feat)
    for o in range(H):
        yy, xx = o * pieces // X, o * pieces % X
        term = mm_nt(attn, wt[yy, xx : xx + pieces].reshape(pieces * wc, feat))
        ht[o & 1, o >> 1, 0:group] = term[:, :HD].astype(BF)
        for i in range(Z):
            ht[o & 1, o >> 1, group:, i * extra : (i + 1) * extra] = term[i * CAP : (i + 1) * CAP, HD:].astype(BF)
    sc = copies(lambda d: (ht.at[1 - (h & 1)], hc), cp, [1])
    start(sc)
    arrive(sc)
    hs[...] = (ht[h & 1].astype(F32) + hc[...].astype(F32)).astype(BF)
    sh = copies(lambda d: (hs.at[((h >> 1) + d) & (H // 2 - 1)], hr.at[d - 1]), hp, every_h)
    start(sh)
    proj = hs[h >> 1].astype(F32)
    for d in every_h:
        arrive(sh[d - 1 : d])
        proj = proj + hr[d - 1].astype(F32)
    lane = iota((CAP, HD), 1)
    for i in range(Z):
        zs[i, 0:CAP] = proj[i * CAP : (i + 1) * CAP].astype(BF)
        zs[i, CAP:] = jnp.where((lane >= i * extra) & (lane < (i + 1) * extra), proj[group:], 0.0).astype(BF)

    sz = copies(lambda d: (zs.at[(z + d) & (Z - 1)], zr.at[d - 1]), zp, every_z)
    start(sz)

    def place(rows, zz):
        l, c = iota((HD, feat), 0), iota((HD, feat), 1)
        p1 = l
        p2 = HD + l - z * extra
        t1 = jnp.where(p1 >= wc, (Z - 1) * wc, 0) + zz * wc + p1
        t2 = jnp.where(p2 >= wc, (Z - 1) * wc, 0) + zz * wc + p2
        inside = (l >= z * extra) & (l < (z + 1) * extra)
        return mm(rows[0:CAP], onehot(c == t1)) + mm(rows[CAP:], onehot((c == t2) & inside))

    rows = place(zs[z], z)
    for d in every_z:
        arrive(sz[d - 1 : d])
        rows = rows + place(zr[d - 1], (z - d) & (Z - 1))
    loads[7].wait()
    loads[8].wait()
    grown = mm(expand[...], rows.astype(BF))
    live = mm(expand[...], jnp.ones((CAP, feat), BF)) > 0.5
    out_ref[...] = jnp.where(live, hid_ref[...].astype(F32) + grown, cac_ref[...].astype(F32)).astype(BF)
    for c in every:
        c.wait_send()


def shards(queries, keys, values, hidden, cached, active, w_out):
    tok, feat = queries.shape
    wc = w_out.shape[1]
    fa, fb = NA * HD, NB * HD
    wa, wb = fa + HD, fb + HD
    group = Z * CAP
    n_copies = 120
    vmem = pltpu.VMEM
    scratch = [
        vmem((tok, feat), BF),
        vmem((tok, feat), BF),
        vmem((tok, feat), BF),
        vmem((1, tok), jnp.int32),
        vmem((X, tok, fa), BF),
        vmem((X, tok, fa), BF),
        vmem((Y, tok, fb), BF),
        vmem((Y, tok, fb), BF),
        vmem((Y, Z, CAP, fa), BF),
        vmem((X, Z, CAP, fb), BF),
        vmem((Y, X, wc, feat), BF),
        vmem((HD, fa), BF),
        vmem((tok, CAP), BF),
        vmem((Y, NA, group, 2 * HD), F32),
        vmem((Y, NA, group, HD), F32),
        vmem((X, NB, group, 2 * HD), F32),
        vmem((X, NB, group, HD), F32),
        vmem((Y, Z, CAP, wa), BF),
        vmem((X, Z, CAP, wb), BF),
        vmem((max(Y - 1, 1), Z, CAP, wa), BF),
        vmem((max(X - 1, 1), Z, CAP, wb), BF),
        vmem((Z, CAP, wa), BF),
        vmem((Z, CAP, wb), BF),
        vmem((Z - 1, CAP, wa), BF),
        vmem((Z - 1, CAP, wb), BF),
        vmem((Z, CAP, feat), BF),
        vmem((2, H // 2, group + CAP, HD), BF),
        vmem((H // 2, group + CAP, HD), BF),
        vmem((H // 2, group + CAP, HD), BF),
        vmem((max(H // 2 - 1, 1), group + CAP, HD), BF),
        vmem((Z, 2 * CAP, HD), BF),
        vmem((Z - 1, 2 * CAP, HD), BF),
        pltpu.SemaphoreType.DMA((n_copies,)),
        pltpu.SemaphoreType.DMA((n_copies,)),
        pltpu.SemaphoreType.DMA((9,)),
    ]
    return pl.pallas_call(
        body,
        out_shape=jax.ShapeDtypeStruct((tok, feat), BF),
        in_specs=[pl.BlockSpec(memory_space=pl.ANY)] * 7,
        out_specs=pl.BlockSpec(memory_space=pltpu.VMEM),
        scratch_shapes=scratch,
        compiler_params=pltpu.CompilerParams(
            collective_id=0, has_side_effects=True, vmem_limit_bytes=60 * 2**20
        ),
    )(queries, keys, values, hidden, cached, active.reshape(1, tok), w_out.T)


def solution(mesh):
    placed = (
        P("seq", "head"),
        P("seq", "head"),
        P("seq", "head"),
        P("seq", "head"),
        P("seq", "head"),
        P("seq"),
        P("head", "seq"),
    )
    return jax.shard_map(
        shards, mesh=mesh, in_specs=placed, out_specs=P("seq", "head"), check_vma=False
    )
```

```python
import math

import jax
import jax.numpy as jnp
from jax import lax
from jax.experimental import pallas as pl
from jax.experimental.pallas import tpu as pltpu
from jax.sharding import PartitionSpec as P

X, Y, Z, H = 4, 4, 4, 8
HD = 128
CAP = 32
BF = jnp.bfloat16
F32 = jnp.float32
NA, NB = 3, 2
MESH = pl.DeviceIdType.MESH


def log2(n):
    return n.bit_length() - 1


def iota(shape, dim):
    return lax.broadcasted_iota(jnp.int32, shape, dim)


def onehot(cond):
    return jnp.where(cond, 1.0, 0.0).astype(BF)


def log2_of(v):
    return jnp.log(v) * (1.0 / math.log(2.0))


def mm(a, b):
    return jnp.dot(a, b, preferred_element_type=F32)


def mm_nt(a, b):
    return lax.dot_general(a, b, (((1,), (1,)), ((), ())), preferred_element_type=F32)


def pack_stat(tile):
    lane = iota(tile.shape, 1)
    hi = tile.astype(BF).astype(F32)
    rest = tile - hi
    mid = rest.astype(BF).astype(F32)
    low = rest - mid
    return jnp.where(lane < 8, hi, jnp.where(lane < 16, mid, jnp.where(lane < 24, low, 0.0))).astype(BF)


def merge(sources, heads, sel):
    width = heads * HD
    logs = [mm(s[:, width:], sel[:, :width]) for s in sources]
    top = logs[0]
    for part in logs[1:]:
        top = jnp.maximum(top, part)
    total, mixed = None, None
    for s, part in zip(sources, logs):
        w = lax.exp2(part - top)
        term = w * s[:, :width].astype(F32)
        total = w if total is None else total + w
        mixed = term if mixed is None else mixed + term
    return mixed / total, top + log2_of(total)


def stat_of(logs, heads):
    lane = iota((logs.shape[0], HD), 1)
    tile = jnp.zeros((logs.shape[0], HD), F32)
    for h in range(heads):
        tile = jnp.where((lane & 7) == h, logs[:, h * HD : (h + 1) * HD], tile)
    return pack_stat(tile)


def body(
    q_hbm, k_hbm, v_hbm, hid_hbm, cac_hbm, act_hbm, w_hbm, out_ref,
    q_ref, hid_ref, cac_ref, act_ref,
    ka, va, kb, vb, qa, qb, wt, sel, expand,
    sum_a, peak_a, sum_b, peak_b,
    pa, pb, ra, rb, a2, b2, ra2, rb2, at,
    ht, hc, hs, hr, zs, zr, base, places, send_sem, recv_sem, load_sem,
):
    tok, feat = q_ref.shape
    wc = w_hbm.shape[0]
    half = NA * HD
    me, h = lax.axis_index("seq"), lax.axis_index("head")
    z = me & (Z - 1)
    x = (me >> log2(Z)) & (X - 1)
    y = me >> log2(Z * X)

    def xp(d):
        return (y * X + ((x + d) & (X - 1))) * Z + z, h

    def yp(d):
        return (((y + d) & (Y - 1)) * X + x) * Z + z, h

    def zp(d):
        return (y * X + x) * Z + ((z + d) & (Z - 1)), h

    def cp(d):
        return me, h ^ 1

    def hp(d):
        return me, (((h >> 1) + d) & (H // 2 - 1)) * 2 + (h & 1)

    barrier = pltpu.get_barrier_semaphore()
    peers = (
        [xp(d) for d in range(1, X)] + [yp(d) for d in range(1, Y)] + [zp(d) for d in range(1, Z)] + [hp(d) for d in range(1, H // 2)] + [cp(1)]
    )
    for p in peers:
        pl.semaphore_signal(barrier, inc=1, device_id=p, device_id_type=MESH)

    lo, hi = pl.ds(0, half), pl.ds(half, feat - half)
    loads = [
        pltpu.make_async_copy(src, dst, load_sem.at[i])
        for i, (src, dst) in enumerate(
            [
                (act_hbm, act_ref), (q_hbm, q_ref),
                (k_hbm.at[:, lo], ka.at[x]), (k_hbm.at[:, hi], kb.at[y]),
                (v_hbm.at[:, lo], va.at[x]), (v_hbm.at[:, hi], vb.at[y]),
                (w_hbm, wt.at[y, x]), (hid_hbm, hid_ref), (cac_hbm, cac_ref),
            ]
        )
    ]
    for c in loads:
        c.start()

    counter = [0]
    every = []

    def copies(make, peer, steps):
        found = []
        for d in steps:
            i = counter[0]
            counter[0] += 1
            src, dst = make(d)
            found.append(
                pltpu.make_async_remote_copy(
                    src_ref=src, dst_ref=dst, send_sem=send_sem.at[i], recv_sem=recv_sem.at[i],
                    device_id=peer(d), device_id_type=MESH,
                )
            )
        return found

    def start(cs):
        for c in cs:
            c.start()
        every.extend(cs)

    def arrive(cs):
        for c in cs:
            c.wait_recv()

    def near(n):
        return [1, n - 1] if n > 2 else list(range(1, n))

    def far(n):
        return list(range(2, n - 1))

    def relay(block, peer, n, at_):
        if n <= 3:
            return []
        on = copies(lambda d: (block((at_ - 1) & (n - 1), 0),) * 2, peer, [1])
        return on + copies(lambda d: (block((at_ + 1) & (n - 1), 1),) * 2, peer, [n - 1])

    every_x, every_y, every_z, every_h = range(1, X), range(1, Y), range(1, Z), range(1, H // 2)

    pl.semaphore_wait(barrier, len(peers))

    parts = [pl.ds(0, tok // 2), pl.ds(tok // 2, tok // 2)]

    def near_copies(src, cols, dst, at_, peer, n, second):
        found = []
        for d in near(n):
            rows = parts[int(d != 1) ^ second]
            found += copies(lambda _: (src.at[rows, cols], dst.at[at_, rows]), peer, [d])
        return found

    ka1, va1, kb1, vb1 = ([
        near_copies(src, cols, dst, at_, peer, n, second) for second in (0, 1)
    ] for src, cols, dst, at_, peer, n in (
        (k_hbm, lo, ka, x, xp, X), (v_hbm, lo, va, x, xp, X), (k_hbm, hi, kb, y, yp, Y), (v_hbm, hi, vb, y, yp, Y),
    ))
    for i in range(2):
        start(ka1[i])
        start(kb1[i])
        start(va1[i])
        start(vb1[i])

    loads[0].wait()
    act = act_ref[...]
    act8 = jnp.broadcast_to(act, (8, tok)).astype(F32).astype(BF)
    before = onehot(iota((tok, tok), 0) < iota((tok, tok), 1))
    rank = mm(act8, before)[0:1, :]
    pick = onehot((iota((CAP, tok), 0).astype(F32) == rank) & (act > 0))
    loads[1].wait()
    own = mm(pick, q_ref[...]).astype(BF)
    qa[y, z] = own[:, :half]
    qb[x, z] = own[:, half:]
    az = copies(lambda d: (qa.at[y, z],) * 2, zp, every_z)
    bz = copies(lambda d: (qb.at[x, z],) * 2, zp, every_z)
    start(az)
    start(bz)

    expand[...] = mm_nt(onehot(iota((tok, tok), 0) == iota((tok, tok), 1)), pick).astype(BF)
    lane, col = iota((HD, half), 0), iota((HD, half), 1)
    sel[...] = onehot(((lane & 7) == (col >> log2(HD))) & (lane < 24))

    for c in loads[2:]:
        c.wait()
    live = mm(expand[...], jnp.ones((CAP, feat), BF)) > 0.5
    base[...] = jnp.where(live, hid_ref[...].astype(F32), cac_ref[...].astype(F32)).astype(BF)
    pieces = X * Y // H
    extra = pieces * wc - HD
    l, c = iota((2 * HD, feat), 0), iota((2 * HD, feat), 1)
    piece = jnp.where(l < HD, l, l - z * extra)
    mine = (l < HD) | ((l >= HD + z * extra) & (l < HD + (z + 1) * extra))
    goal = jnp.where(piece >= wc, (Z - 1) * wc, 0) + piece
    for d in range(Z):
        places[d] = onehot((goal + ((z - d) & (Z - 1)) * wc == c) & mine)
    ay = copies(lambda d: (qa.at[y],) * 2, yp, every_y)
    bx = copies(lambda d: (qb.at[x],) * 2, xp, every_x)
    ka2 = relay(lambda i, part: ka.at[i, parts[part]], xp, X, x)
    va2 = relay(lambda i, part: va.at[i, parts[part]], xp, X, x)
    kb2 = relay(lambda i, part: kb.at[i, parts[part]], yp, Y, y)
    vb2 = relay(lambda i, part: vb.at[i, parts[part]], yp, Y, y)
    arrive(az)
    start(ay)
    arrive(bz)
    start(bx)
    arrive(ka1[0])
    start(ka2)
    arrive(kb1[0])
    start(kb2)
    arrive(va1[0])
    start(va2)
    arrive(vb1[0])
    start(vb2)
    arrive(ka1[1])
    arrive(va1[1])

    cut = [pl.ds(0, 48), pl.ds(48, wc - 48)]
    wy0 = copies(lambda d: (wt.at[y, x, :, lo],) * 2, yp, every_y)
    wx1 = copies(lambda d: (wt.at[y, x, :, hi],) * 2, xp, every_x)
    wx0 = copies(lambda d: (wt.at[:, x, :, lo],) * 2, xp, near(X))
    wy1 = copies(lambda d: (wt.at[y, :, :, hi],) * 2, yp, near(Y))
    wx0 = [wx0, relay(lambda i, part: wt.at[:, i, cut[part], lo], xp, X, x)]
    wy1 = [wy1, relay(lambda i, part: wt.at[i, :, cut[part], hi], yp, Y, y)]

    scale = 1.0 / (HD**0.5 * math.log(2.0))
    ones = jnp.ones((tok, HD), BF)
    group = Z * CAP

    def attend(heads, rows, k, v, blocks, sums, peaks, dest, first, last):
        @pl.loop(0, rows.shape[0])
        def _(g):
            lane = iota((group, HD), 1)
            tile = jnp.zeros((group, HD), F32)
            for i in range(heads):
                c = slice(i * HD, (i + 1) * HD)
                query = rows[g, :, :, c].reshape(group, HD)
                scores = [mm_nt(query, k[b, :, c]) * scale for b in blocks]
                peak = jnp.max(scores[0], axis=1, keepdims=True)
                for score in scores[1:]:
                    peak = jnp.maximum(peak, jnp.max(score, axis=1, keepdims=True))
                if not first:
                    old = peaks[g, i]
                    peak = jnp.maximum(old, peak)
                both = None
                for b, score in zip(blocks, scores):
                    expo = lax.exp2(score - peak[:, 0:1]).astype(BF)
                    part = mm(expo, jnp.concatenate([v[b, :, c], ones], axis=1))
                    both = part if both is None else both + part
                if not first:
                    fade = lax.exp2(old - peak)
                    both = both + sums[g, i] * jnp.concatenate([fade, fade], axis=1)
                if last:
                    total = both[:, HD:]
                    dest[g, :, :, c] = (both[:, :HD] / total).astype(BF).reshape(Z, CAP, HD)
                    tile = jnp.where((lane & 7) == i, peak + log2_of(total), tile)
                else:
                    sums[g, i] = both
                    peaks[g, i] = jnp.broadcast_to(peak, (group, HD))
            if last:
                dest[g, :, :, heads * HD :] = pack_stat(tile).reshape(Z, CAP, HD)

    def near_blocks(at_, n):
        return [at_] + [(at_ - d) & (n - 1) for d in near(n)]

    def far_blocks(at_, n):
        return [(at_ - d) & (n - 1) for d in far(n)]

    arrive(ay)
    attend(NA, qa, ka, va, near_blocks(x, X), sum_a, peak_a, pa, True, X <= 3)
    arrive(bx)
    arrive(kb1[1])
    arrive(vb1[1])
    attend(NB, qb, kb, vb, near_blocks(y, Y), sum_b, peak_b, pb, True, Y <= 3)
    arrive(ka2)
    arrive(va2)
    if X > 3:
        attend(NA, qa, ka, va, far_blocks(x, X), sum_a, peak_a, pa, False, True)
    sa = copies(lambda d: (pa.at[(y + d) & (Y - 1)], ra.at[d - 1]), yp, every_y)
    start(sa)
    arrive(kb2)
    arrive(vb2)
    if Y > 3:
        attend(NB, qb, kb, vb, far_blocks(y, Y), sum_b, peak_b, pb, False, True)
    sb = copies(lambda d: (pb.at[(x + d) & (X - 1)], rb.at[d - 1]), xp, every_x)
    start(sb)
    start(wy0)
    start(wx1)

    arrive(sa)

    @pl.loop(0, Z)
    def _(i):
        mean, logs = merge([pa[y, i]] + [ra[d, i] for d in range(Y - 1)], NA, sel[...])
        a2[i, :, :half] = mean.astype(BF)
        a2[i, :, half:] = stat_of(logs, NA)

    sa2 = copies(lambda d: (a2.at[(z + d) & (Z - 1)], ra2.at[d - 1]), zp, every_z)
    start(sa2)
    arrive(wx1)
    start(wy1[0])
    arrive(sb)

    @pl.loop(0, Z)
    def _(i):
        mean, logs = merge([pb[x, i]] + [rb[d, i] for d in range(X - 1)], NB, sel[...])
        b2[i, :, : NB * HD] = mean.astype(BF)
        b2[i, :, NB * HD :] = stat_of(logs, NB)

    sb2 = copies(lambda d: (b2.at[(z + d) & (Z - 1)], rb2.at[d - 1]), zp, every_z)
    start(sb2)
    arrive(wy0)
    start(wx0[0])
    arrive(sa2)
    at[z, :, :half] = merge([a2[z]] + [ra2[d] for d in range(Z - 1)], NA, sel[...])[0].astype(BF)
    arrive(sb2)
    at[z, :, half:] = merge([b2[z]] + [rb2[d] for d in range(Z - 1)], NB, sel[...])[0].astype(BF)
    tz = copies(lambda d: (at.at[z],) * 2, zp, every_z)
    start(tz)
    arrive(wy1[0])
    start(wy1[1])
    arrive(wx0[0])
    start(wx0[1])
    arrive(tz)
    arrive(wx0[1])
    arrive(wy1[1])

    attn = at[...].reshape(group, feat)
    for o in range(H):
        yy, xx = o * pieces // X, o * pieces % X
        term = mm_nt(attn, wt[yy, xx : xx + pieces].reshape(pieces * wc, feat))
        ht[o & 1, o >> 1, 0:group] = term[:, :HD].astype(BF)
        for i in range(Z):
            ht[o & 1, o >> 1, group:, i * extra : (i + 1) * extra] = term[i * CAP : (i + 1) * CAP, HD:].astype(BF)
    sc = copies(lambda d: (ht.at[1 - (h & 1)], hc), cp, [1])
    start(sc)
    arrive(sc)
    hs[...] = (ht[h & 1].astype(F32) + hc[...].astype(F32)).astype(BF)
    sh = copies(lambda d: (hs.at[((h >> 1) + d) & (H // 2 - 1)], hr.at[d - 1]), hp, every_h)
    start(sh)
    proj = hs[h >> 1].astype(F32)
    for d in every_h:
        arrive(sh[d - 1 : d])
        proj = proj + hr[d - 1].astype(F32)
    lane = iota((CAP, HD), 1)
    for i in range(Z):
        zs[i, :, :HD] = proj[i * CAP : (i + 1) * CAP].astype(BF)
        zs[i, :, HD:] = jnp.where((lane >= i * extra) & (lane < (i + 1) * extra), proj[group:], 0.0).astype(BF)

    sz = copies(lambda d: (zs.at[(z + d) & (Z - 1)], zr.at[d - 1]), zp, every_z)
    start(sz)

    rows = mm(zs[z], places[0])
    for d in every_z:
        arrive(sz[d - 1 : d])
        rows = rows + mm(zr[d - 1], places[d])
    out_ref[...] = (base[...].astype(F32) + mm(expand[...], rows.astype(BF))).astype(BF)
    for c in every:
        c.wait_send()


def shards(queries, keys, values, hidden, cached, active, w_out):
    tok, feat = queries.shape
    wc = w_out.shape[1]
    fa, fb = NA * HD, NB * HD
    wa, wb = fa + HD, fb + HD
    group = Z * CAP
    n_copies = 120
    vmem = pltpu.VMEM
    scratch = [
        vmem((tok, feat), BF),
        vmem((tok, feat), BF),
        vmem((tok, feat), BF),
        vmem((1, tok), jnp.int32),
        vmem((X, tok, fa), BF),
        vmem((X, tok, fa), BF),
        vmem((Y, tok, fb), BF),
        vmem((Y, tok, fb), BF),
        vmem((Y, Z, CAP, fa), BF),
        vmem((X, Z, CAP, fb), BF),
        vmem((Y, X, wc, feat), BF),
        vmem((HD, fa), BF),
        vmem((tok, CAP), BF),
        vmem((Y, NA, group, 2 * HD), F32),
        vmem((Y, NA, group, HD), F32),
        vmem((X, NB, group, 2 * HD), F32),
        vmem((X, NB, group, HD), F32),
        vmem((Y, Z, CAP, wa), BF),
        vmem((X, Z, CAP, wb), BF),
        vmem((max(Y - 1, 1), Z, CAP, wa), BF),
        vmem((max(X - 1, 1), Z, CAP, wb), BF),
        vmem((Z, CAP, wa), BF),
        vmem((Z, CAP, wb), BF),
        vmem((Z - 1, CAP, wa), BF),
        vmem((Z - 1, CAP, wb), BF),
        vmem((Z, CAP, feat), BF),
        vmem((2, H // 2, group + CAP, HD), BF),
        vmem((H // 2, group + CAP, HD), BF),
        vmem((H // 2, group + CAP, HD), BF),
        vmem((max(H // 2 - 1, 1), group + CAP, HD), BF),
        vmem((Z, CAP, 2 * HD), BF),
        vmem((Z - 1, CAP, 2 * HD), BF),
        vmem((tok, feat), BF),
        vmem((Z, 2 * HD, feat), BF),
        pltpu.SemaphoreType.DMA((n_copies,)),
        pltpu.SemaphoreType.DMA((n_copies,)),
        pltpu.SemaphoreType.DMA((9,)),
    ]
    return pl.pallas_call(
        body,
        out_shape=jax.ShapeDtypeStruct((tok, feat), BF),
        in_specs=[pl.BlockSpec(memory_space=pl.ANY)] * 7,
        out_specs=pl.BlockSpec(memory_space=pltpu.VMEM),
        scratch_shapes=scratch,
        compiler_params=pltpu.CompilerParams(
            collective_id=0, has_side_effects=True, vmem_limit_bytes=60 * 2**20
        ),
    )(queries, keys, values, hidden, cached, active.reshape(1, tok), w_out.T)


def solution(mesh):
    placed = (
        P("seq", "head"),
        P("seq", "head"),
        P("seq", "head"),
        P("seq", "head"),
        P("seq", "head"),
        P("seq"),
        P("head", "seq"),
    )
    return jax.shard_map(
        shards, mesh=mesh, in_specs=placed, out_specs=P("seq", "head"), check_vma=False
    )
```

```python
import math

import jax
import jax.numpy as jnp
from jax import lax
from jax.experimental import pallas as pl
from jax.experimental.pallas import tpu as pltpu
from jax.sharding import PartitionSpec as P

X, Y, Z, H = 4, 4, 4, 8
HD = 128
CAP = 32
BF = jnp.bfloat16
F32 = jnp.float32
NA, NB = 3, 2
MESH = pl.DeviceIdType.MESH


def log2(n):
    return n.bit_length() - 1


def iota(shape, dim):
    return lax.broadcasted_iota(jnp.int32, shape, dim)


def onehot(cond):
    return jnp.where(cond, 1.0, 0.0).astype(BF)


def log2_of(v):
    return jnp.log(v) * (1.0 / math.log(2.0))


def mm(a, b):
    return jnp.dot(a, b, preferred_element_type=F32)


def mm_nt(a, b):
    return lax.dot_general(a, b, (((1,), (1,)), ((), ())), preferred_element_type=F32)


def pack_stat(tile):
    lane = iota(tile.shape, 1)
    hi = tile.astype(BF).astype(F32)
    rest = tile - hi
    mid = rest.astype(BF).astype(F32)
    low = rest - mid
    return jnp.where(lane < 8, hi, jnp.where(lane < 16, mid, jnp.where(lane < 24, low, 0.0))).astype(BF)


def merge(sources, heads, sel):
    width = heads * HD
    logs = [mm(s[:, width:], sel[:, :width]) for s in sources]
    top = logs[0]
    for part in logs[1:]:
        top = jnp.maximum(top, part)
    total, mixed = None, None
    for s, part in zip(sources, logs):
        w = lax.exp2(part - top)
        term = w * s[:, :width].astype(F32)
        total = w if total is None else total + w
        mixed = term if mixed is None else mixed + term
    return mixed / total, top + log2_of(total)


def stat_of(logs, heads):
    lane = iota((logs.shape[0], HD), 1)
    tile = jnp.zeros((logs.shape[0], HD), F32)
    for h in range(heads):
        tile = jnp.where((lane & 7) == h, logs[:, h * HD : (h + 1) * HD], tile)
    return pack_stat(tile)


def body(
    q_hbm, k_hbm, v_hbm, hid_hbm, cac_hbm, act_hbm, w_hbm, out_ref,
    q_ref, hid_ref, cac_ref, act_ref,
    ka, va, kb, vb, qa, qb, wt, sel, expand,
    sum_a, peak_a, sum_b, peak_b,
    pa, pb, ra, rb, a2, b2, ra2, rb2, at,
    ht, hc, hs, hr, zs, zr, base, places, send_sem, recv_sem, load_sem,
):
    tok, feat = q_ref.shape
    wc = w_hbm.shape[0]
    half = NA * HD
    me, h = lax.axis_index("seq"), lax.axis_index("head")
    z = me & (Z - 1)
    x = (me >> log2(Z)) & (X - 1)
    y = me >> log2(Z * X)

    def xp(d):
        return (y * X + ((x + d) & (X - 1))) * Z + z, h

    def yp(d):
        return (((y + d) & (Y - 1)) * X + x) * Z + z, h

    def zp(d):
        return (y * X + x) * Z + ((z + d) & (Z - 1)), h

    def cp(d):
        return me, h ^ 1

    def hp(d):
        return me, (((h >> 1) + d) & (H // 2 - 1)) * 2 + (h & 1)

    barrier = pltpu.get_barrier_semaphore()
    peers = (
        [xp(d) for d in range(1, X)] + [yp(d) for d in range(1, Y)] + [zp(d) for d in range(1, Z)] + [hp(d) for d in range(1, H // 2)] + [cp(1)]
    )
    for p in peers:
        pl.semaphore_signal(barrier, inc=1, device_id=p, device_id_type=MESH)

    lo, hi = pl.ds(0, half), pl.ds(half, feat - half)
    loads = [
        pltpu.make_async_copy(src, dst, load_sem.at[i])
        for i, (src, dst) in enumerate(
            [
                (act_hbm, act_ref), (q_hbm, q_ref),
                (k_hbm.at[:, lo], ka.at[x]), (k_hbm.at[:, hi], kb.at[y]),
                (v_hbm.at[:, lo], va.at[x]), (v_hbm.at[:, hi], vb.at[y]),
                (w_hbm, wt.at[y, x]), (hid_hbm, hid_ref), (cac_hbm, cac_ref),
            ]
        )
    ]
    for c in loads:
        c.start()

    counter = [0]
    every = []

    def copies(make, peer, steps):
        found = []
        for d in steps:
            i = counter[0]
            counter[0] += 1
            src, dst = make(d)
            found.append(
                pltpu.make_async_remote_copy(
                    src_ref=src, dst_ref=dst, send_sem=send_sem.at[i], recv_sem=recv_sem.at[i],
                    device_id=peer(d), device_id_type=MESH,
                )
            )
        return found

    def start(cs):
        for c in cs:
            c.start()
        every.extend(cs)

    def arrive(cs):
        for c in cs:
            c.wait_recv()

    def near(n):
        return [1, n - 1] if n > 2 else list(range(1, n))

    def far(n):
        return list(range(2, n - 1))

    def relay(block, peer, n, at_):
        if n <= 3:
            return []
        on = copies(lambda d: (block((at_ - 1) & (n - 1), 0),) * 2, peer, [1])
        return on + copies(lambda d: (block((at_ + 1) & (n - 1), 1),) * 2, peer, [n - 1])

    every_x, every_y, every_z, every_h = range(1, X), range(1, Y), range(1, Z), range(1, H // 2)

    pl.semaphore_wait(barrier, len(peers))

    parts = [pl.ds(0, tok // 2), pl.ds(tok // 2, tok // 2)]

    def near_copies(src, cols, dst, at_, peer, n, second):
        found = []
        for d in near(n):
            rows = parts[int(d != 1) ^ second]
            found += copies(lambda _: (src.at[rows, cols], dst.at[at_, rows]), peer, [d])
        return found

    ka1, va1, kb1, vb1 = ([
        near_copies(src, cols, dst, at_, peer, n, second) for second in (0, 1)
    ] for src, cols, dst, at_, peer, n in (
        (k_hbm, lo, ka, x, xp, X), (v_hbm, lo, va, x, xp, X), (k_hbm, hi, kb, y, yp, Y), (v_hbm, hi, vb, y, yp, Y),
    ))
    for c in (ka1[0], kb1[0], va1[0], vb1[0], ka1[1], kb1[1]):
        start(c)

    loads[0].wait()
    act = act_ref[...]
    act8 = jnp.broadcast_to(act, (8, tok)).astype(F32).astype(BF)
    before = onehot(iota((tok, tok), 0) < iota((tok, tok), 1))
    rank = mm(act8, before)[0:1, :]
    pick = onehot((iota((CAP, tok), 0).astype(F32) == rank) & (act > 0))
    loads[1].wait()
    own = mm(pick, q_ref[...]).astype(BF)
    qa[y, z] = own[:, :half]
    qb[x, z] = own[:, half:]
    az = copies(lambda d: (qa.at[y, z],) * 2, zp, every_z)
    bz = copies(lambda d: (qb.at[x, z],) * 2, zp, every_z)
    start(az)
    start(bz)

    expand[...] = mm_nt(onehot(iota((tok, tok), 0) == iota((tok, tok), 1)), pick).astype(BF)
    lane, col = iota((HD, half), 0), iota((HD, half), 1)
    sel[...] = onehot(((lane & 7) == (col >> log2(HD))) & (lane < 24))

    for c in loads[2:]:
        c.wait()
    ay = copies(lambda d: (qa.at[y],) * 2, yp, every_y)
    bx = copies(lambda d: (qb.at[x],) * 2, xp, every_x)
    ka2 = relay(lambda i, part: ka.at[i, parts[part]], xp, X, x)
    va2 = relay(lambda i, part: va.at[i, parts[part]], xp, X, x)
    kb2 = relay(lambda i, part: kb.at[i, parts[part]], yp, Y, y)
    vb2 = relay(lambda i, part: vb.at[i, parts[part]], yp, Y, y)
    arrive(az)
    start(ay)
    arrive(bz)
    start(bx)
    start(va1[1])
    start(vb1[1])
    arrive(ka1[0])
    start(ka2)
    arrive(kb1[0])
    start(kb2)
    arrive(va1[0])
    start(va2)
    arrive(vb1[0])
    start(vb2)
    arrive(ka1[1])
    arrive(va1[1])

    cut = [pl.ds(0, 48), pl.ds(48, wc - 48)]
    wy0 = copies(lambda d: (wt.at[y, x, :, lo],) * 2, yp, every_y)
    wx1 = copies(lambda d: (wt.at[y, x, :, hi],) * 2, xp, every_x)
    wx0 = copies(lambda d: (wt.at[:, x, :, lo],) * 2, xp, near(X))
    wy1 = copies(lambda d: (wt.at[y, :, :, hi],) * 2, yp, near(Y))
    wx0 = [wx0, relay(lambda i, part: wt.at[:, i, cut[part], lo], xp, X, x)]
    wy1 = [wy1, relay(lambda i, part: wt.at[i, :, cut[part], hi], yp, Y, y)]

    scale = 1.0 / (HD**0.5 * math.log(2.0))
    ones = jnp.ones((tok, HD), BF)
    group = Z * CAP

    def attend(heads, rows, k, v, blocks, sums, peaks, dest, first, last):
        lines = rows.shape[0]
        plane = lines * group
        lane = iota((plane, HD), 1)
        tile = jnp.zeros((plane, HD), F32)
        for i in range(heads):
            c = slice(i * HD, (i + 1) * HD)
            query = rows[:, :, :, c].reshape(plane, HD)
            scores = [mm_nt(query, k[b, :, c]) * scale for b in blocks]
            peak = jnp.max(scores[0], axis=1, keepdims=True)
            for score in scores[1:]:
                peak = jnp.maximum(peak, jnp.max(score, axis=1, keepdims=True))
            if not first:
                old = peaks[i]
                peak = jnp.maximum(old, peak)
            both = None
            for b, score in zip(blocks, scores):
                expo = lax.exp2(score - peak[:, 0:1]).astype(BF)
                part = mm(expo, jnp.concatenate([v[b, :, c], ones], axis=1))
                both = part if both is None else both + part
            if not first:
                fade = lax.exp2(old - peak)
                both = both + sums[i] * jnp.concatenate([fade, fade], axis=1)
            if last:
                total = both[:, HD:]
                dest[:, :, :, c] = (both[:, :HD] / total).astype(BF).reshape(lines, Z, CAP, HD)
                tile = jnp.where((lane & 7) == i, peak + log2_of(total), tile)
            else:
                sums[i] = both
                peaks[i] = jnp.broadcast_to(peak, (plane, HD))
        if last:
            dest[:, :, :, heads * HD :] = pack_stat(tile).reshape(lines, Z, CAP, HD)

    def near_blocks(at_, n):
        return [at_] + [(at_ - d) & (n - 1) for d in near(n)]

    def far_blocks(at_, n):
        return [(at_ - d) & (n - 1) for d in far(n)]

    arrive(ay)
    attend(NA, qa, ka, va, near_blocks(x, X), sum_a, peak_a, pa, True, X <= 3)
    arrive(bx)
    arrive(kb1[1])
    arrive(vb1[1])
    attend(NB, qb, kb, vb, near_blocks(y, Y), sum_b, peak_b, pb, True, Y <= 3)
    start(wy0)
    start(wx1)
    arrive(ka2)
    arrive(va2)
    if X > 3:
        attend(NA, qa, ka, va, far_blocks(x, X), sum_a, peak_a, pa, False, True)
    sa = copies(lambda d: (pa.at[(y + d) & (Y - 1)], ra.at[d - 1]), yp, every_y)
    start(sa)
    arrive(kb2)
    arrive(vb2)
    if Y > 3:
        attend(NB, qb, kb, vb, far_blocks(y, Y), sum_b, peak_b, pb, False, True)
    sb = copies(lambda d: (pb.at[(x + d) & (X - 1)], rb.at[d - 1]), xp, every_x)
    start(sb)
    live = mm(expand[...], jnp.ones((CAP, feat), BF)) > 0.5
    base[...] = jnp.where(live, hid_ref[...].astype(F32), cac_ref[...].astype(F32)).astype(BF)
    pieces = X * Y // H
    extra = pieces * wc - HD
    l, c = iota((2 * HD, feat), 0), iota((2 * HD, feat), 1)
    piece = jnp.where(l < HD, l, l - z * extra)
    mine = (l < HD) | ((l >= HD + z * extra) & (l < HD + (z + 1) * extra))
    goal = jnp.where(piece >= wc, (Z - 1) * wc, 0) + piece
    for d in range(Z):
        places[d] = onehot((goal + ((z - d) & (Z - 1)) * wc == c) & mine)
    arrive(wy0)
    arrive(wx1)
    start(wx0[0])
    start(wy1[0])

    arrive(sa)

    def merge_in(dest, sources, heads):
        mean, logs = merge([r.reshape(group, r.shape[-1]) for r in sources], heads, sel[...])
        dest[:, :, : heads * HD] = mean.astype(BF).reshape(Z, CAP, heads * HD)
        dest[:, :, heads * HD :] = stat_of(logs, heads).reshape(Z, CAP, HD)

    merge_in(a2, [pa[y]] + [ra[d] for d in range(Y - 1)], NA)
    sa2 = copies(lambda d: (a2.at[(z + d) & (Z - 1)], ra2.at[d - 1]), zp, every_z)
    start(sa2)
    arrive(sb)

    merge_in(b2, [pb[x]] + [rb[d] for d in range(X - 1)], NB)
    sb2 = copies(lambda d: (b2.at[(z + d) & (Z - 1)], rb2.at[d - 1]), zp, every_z)
    start(sb2)
    arrive(wx0[0])
    start(wx0[1])
    arrive(wy1[0])
    start(wy1[1])
    arrive(sa2)
    at[z, :, :half] = merge([a2[z]] + [ra2[d] for d in range(Z - 1)], NA, sel[...])[0].astype(BF)
    arrive(sb2)
    at[z, :, half:] = merge([b2[z]] + [rb2[d] for d in range(Z - 1)], NB, sel[...])[0].astype(BF)
    tz = copies(lambda d: (at.at[z],) * 2, zp, every_z)
    start(tz)
    arrive(tz)
    arrive(wx0[1])
    arrive(wy1[1])

    attn = at[...].reshape(group, feat)
    for o in range(H):
        yy, xx = o * pieces // X, o * pieces % X
        term = mm_nt(attn, wt[yy, xx : xx + pieces].reshape(pieces * wc, feat))
        ht[o & 1, o >> 1, 0:group] = term[:, :HD].astype(BF)
        for i in range(Z):
            ht[o & 1, o >> 1, group:, i * extra : (i + 1) * extra] = term[i * CAP : (i + 1) * CAP, HD:].astype(BF)
    sc = copies(lambda d: (ht.at[1 - (h & 1)], hc), cp, [1])
    start(sc)
    arrive(sc)
    hs[...] = (ht[h & 1].astype(F32) + hc[...].astype(F32)).astype(BF)
    sh = copies(lambda d: (hs.at[((h >> 1) + d) & (H // 2 - 1)], hr.at[d - 1]), hp, every_h)
    start(sh)
    proj = hs[h >> 1].astype(F32)
    for d in every_h:
        arrive(sh[d - 1 : d])
        proj = proj + hr[d - 1].astype(F32)
    lane = iota((CAP, HD), 1)
    for i in range(Z):
        zs[i, :, :HD] = proj[i * CAP : (i + 1) * CAP].astype(BF)
        zs[i, :, HD:] = jnp.where((lane >= i * extra) & (lane < (i + 1) * extra), proj[group:], 0.0).astype(BF)

    sz = copies(lambda d: (zs.at[(z + d) & (Z - 1)], zr.at[d - 1]), zp, every_z)
    start(sz)

    rows = mm(zs[z], places[0])
    for d in every_z:
        arrive(sz[d - 1 : d])
        rows = rows + mm(zr[d - 1], places[d])
    out_ref[...] = (base[...].astype(F32) + mm(expand[...], rows.astype(BF))).astype(BF)
    for c in every:
        c.wait_send()


def shards(queries, keys, values, hidden, cached, active, w_out):
    tok, feat = queries.shape
    wc = w_out.shape[1]
    fa, fb = NA * HD, NB * HD
    wa, wb = fa + HD, fb + HD
    group = Z * CAP
    n_copies = 120
    vmem = pltpu.VMEM
    scratch = [
        vmem((tok, feat), BF),
        vmem((tok, feat), BF),
        vmem((tok, feat), BF),
        vmem((1, tok), jnp.int32),
        vmem((X, tok, fa), BF),
        vmem((X, tok, fa), BF),
        vmem((Y, tok, fb), BF),
        vmem((Y, tok, fb), BF),
        vmem((Y, Z, CAP, fa), BF),
        vmem((X, Z, CAP, fb), BF),
        vmem((Y, X, wc, feat), BF),
        vmem((HD, fa), BF),
        vmem((tok, CAP), BF),
        vmem((NA, Y * group, 2 * HD), F32),
        vmem((NA, Y * group, HD), F32),
        vmem((NB, X * group, 2 * HD), F32),
        vmem((NB, X * group, HD), F32),
        vmem((Y, Z, CAP, wa), BF),
        vmem((X, Z, CAP, wb), BF),
        vmem((max(Y - 1, 1), Z, CAP, wa), BF),
        vmem((max(X - 1, 1), Z, CAP, wb), BF),
        vmem((Z, CAP, wa), BF),
        vmem((Z, CAP, wb), BF),
        vmem((Z - 1, CAP, wa), BF),
        vmem((Z - 1, CAP, wb), BF),
        vmem((Z, CAP, feat), BF),
        vmem((2, H // 2, group + CAP, HD), BF),
        vmem((H // 2, group + CAP, HD), BF),
        vmem((H // 2, group + CAP, HD), BF),
        vmem((max(H // 2 - 1, 1), group + CAP, HD), BF),
        vmem((Z, CAP, 2 * HD), BF),
        vmem((Z - 1, CAP, 2 * HD), BF),
        vmem((tok, feat), BF),
        vmem((Z, 2 * HD, feat), BF),
        pltpu.SemaphoreType.DMA((n_copies,)),
        pltpu.SemaphoreType.DMA((n_copies,)),
        pltpu.SemaphoreType.DMA((9,)),
    ]
    return pl.pallas_call(
        body,
        out_shape=jax.ShapeDtypeStruct((tok, feat), BF),
        in_specs=[pl.BlockSpec(memory_space=pl.ANY)] * 7,
        out_specs=pl.BlockSpec(memory_space=pltpu.VMEM),
        scratch_shapes=scratch,
        compiler_params=pltpu.CompilerParams(
            collective_id=0, has_side_effects=True, vmem_limit_bytes=60 * 2**20
        ),
    )(queries, keys, values, hidden, cached, active.reshape(1, tok), w_out.T)


def solution(mesh):
    placed = (
        P("seq", "head"),
        P("seq", "head"),
        P("seq", "head"),
        P("seq", "head"),
        P("seq", "head"),
        P("seq"),
        P("head", "seq"),
    )
    return jax.shard_map(
        shards, mesh=mesh, in_specs=placed, out_specs=P("seq", "head"), check_vma=False
    )
```

```python
import math

import jax
import jax.numpy as jnp
from jax import lax
from jax.experimental import pallas as pl
from jax.experimental.pallas import tpu as pltpu
from jax.sharding import PartitionSpec as P

X, Y, Z, H = 4, 4, 4, 8
HD = 128
CAP = 32
BF = jnp.bfloat16
F32 = jnp.float32
NA, NB = 3, 2
MESH = pl.DeviceIdType.MESH


def log2(n):
    return n.bit_length() - 1


def iota(shape, dim):
    return lax.broadcasted_iota(jnp.int32, shape, dim)


def onehot(cond):
    return jnp.where(cond, 1.0, 0.0).astype(BF)


def log2_of(v):
    return jnp.log(v) * (1.0 / math.log(2.0))


def mm(a, b):
    return jnp.dot(a, b, preferred_element_type=F32)


def mm_nt(a, b):
    return lax.dot_general(a, b, (((1,), (1,)), ((), ())), preferred_element_type=F32)


def pack_stat(tile):
    lane = iota(tile.shape, 1)
    hi = tile.astype(BF).astype(F32)
    rest = tile - hi
    mid = rest.astype(BF).astype(F32)
    low = rest - mid
    return jnp.where(lane < 8, hi, jnp.where(lane < 16, mid, jnp.where(lane < 24, low, 0.0))).astype(BF)


def merge(sources, heads, sel):
    width = heads * HD
    logs = [mm(s[:, width:], sel[:, :width]) for s in sources]
    top = logs[0]
    for part in logs[1:]:
        top = jnp.maximum(top, part)
    total, mixed = None, None
    for s, part in zip(sources, logs):
        w = lax.exp2(part - top)
        term = w * s[:, :width].astype(F32)
        total = w if total is None else total + w
        mixed = term if mixed is None else mixed + term
    return mixed / total, top + log2_of(total)


def stat_of(logs, heads):
    lane = iota((logs.shape[0], HD), 1)
    tile = jnp.zeros((logs.shape[0], HD), F32)
    for h in range(heads):
        tile = jnp.where((lane & 7) == h, logs[:, h * HD : (h + 1) * HD], tile)
    return pack_stat(tile)


def body(
    q_hbm, k_hbm, v_hbm, hid_hbm, cac_hbm, act_hbm, w_hbm, out_ref,
    q_ref, hid_ref, cac_ref, act_ref,
    ka, va, kb, vb, qa, qb, wt, sel, expand,
    sum_a, peak_a, sum_b, peak_b,
    pa, pb, ra, rb, a2, b2, ra2, rb2, at,
    ht, hc, hs, hr, zs, zr, base, places, send_sem, recv_sem, load_sem,
):
    tok, feat = q_ref.shape
    wc = w_hbm.shape[0]
    half = NA * HD
    me, h = lax.axis_index("seq"), lax.axis_index("head")
    z = me & (Z - 1)
    x = (me >> log2(Z)) & (X - 1)
    y = me >> log2(Z * X)

    def xp(d):
        return (y * X + ((x + d) & (X - 1))) * Z + z, h

    def yp(d):
        return (((y + d) & (Y - 1)) * X + x) * Z + z, h

    def zp(d):
        return (y * X + x) * Z + ((z + d) & (Z - 1)), h

    def cp(d):
        return me, h ^ 1

    def hp(d):
        return me, (((h >> 1) + d) & (H // 2 - 1)) * 2 + (h & 1)

    barrier = pltpu.get_barrier_semaphore()
    peers = (
        [xp(d) for d in range(1, X)] + [yp(d) for d in range(1, Y)] + [zp(d) for d in range(1, Z)] + [hp(d) for d in range(1, H // 2)] + [cp(1)]
    )
    for p in peers:
        pl.semaphore_signal(barrier, inc=1, device_id=p, device_id_type=MESH)

    lo, hi = pl.ds(0, half), pl.ds(half, feat - half)
    loads = [
        pltpu.make_async_copy(src, dst, load_sem.at[i])
        for i, (src, dst) in enumerate(
            [
                (act_hbm, act_ref), (q_hbm, q_ref),
                (k_hbm.at[:, lo], ka.at[x]), (k_hbm.at[:, hi], kb.at[y]),
                (v_hbm.at[:, lo], va.at[x]), (v_hbm.at[:, hi], vb.at[y]),
                (w_hbm, wt.at[y, x]), (hid_hbm, hid_ref), (cac_hbm, cac_ref),
            ]
        )
    ]
    for c in loads:
        c.start()

    counter = [0]
    every = []

    def copies(make, peer, steps):
        found = []
        for d in steps:
            i = counter[0]
            counter[0] += 1
            src, dst = make(d)
            found.append(
                pltpu.make_async_remote_copy(
                    src_ref=src, dst_ref=dst, send_sem=send_sem.at[i], recv_sem=recv_sem.at[i],
                    device_id=peer(d), device_id_type=MESH,
                )
            )
        return found

    def start(cs):
        for c in cs:
            c.start()
        every.extend(cs)

    def arrive(cs):
        for c in cs:
            c.wait_recv()

    def near(n):
        return [1, n - 1] if n > 2 else list(range(1, n))

    def far(n):
        return list(range(2, n - 1))

    def relay(block, peer, n, at_):
        if n <= 3:
            return []
        on = copies(lambda d: (block((at_ - 1) & (n - 1), 0),) * 2, peer, [1])
        return on + copies(lambda d: (block((at_ + 1) & (n - 1), 1),) * 2, peer, [n - 1])

    every_x, every_y, every_z, every_h = range(1, X), range(1, Y), range(1, Z), range(1, H // 2)

    pl.semaphore_wait(barrier, len(peers))

    parts = [pl.ds(0, tok // 2), pl.ds(tok // 2, tok // 2)]

    def near_copies(src, cols, dst, at_, peer, n, second):
        found = []
        for d in near(n):
            rows = parts[int(d != 1) ^ second]
            found += copies(lambda _: (src.at[rows, cols], dst.at[at_, rows]), peer, [d])
        return found

    ka1, va1, kb1, vb1 = ([
        near_copies(src, cols, dst, at_, peer, n, second) for second in (0, 1)
    ] for src, cols, dst, at_, peer, n in (
        (k_hbm, lo, ka, x, xp, X), (v_hbm, lo, va, x, xp, X), (k_hbm, hi, kb, y, yp, Y), (v_hbm, hi, vb, y, yp, Y),
    ))
    for c in (ka1[0], kb1[0], va1[0], vb1[0], ka1[1], kb1[1]):
        start(c)

    loads[0].wait()
    act = act_ref[...]
    act8 = jnp.broadcast_to(act, (8, tok)).astype(F32).astype(BF)
    before = onehot(iota((tok, tok), 0) < iota((tok, tok), 1))
    rank = mm(act8, before)[0:1, :]
    pick = onehot((iota((CAP, tok), 0).astype(F32) == rank) & (act > 0))
    loads[1].wait()
    own = mm(pick, q_ref[...]).astype(BF)
    qa[y, z] = own[:, :half]
    qb[x, z] = own[:, half:]
    az = copies(lambda d: (qa.at[y, z],) * 2, zp, every_z)
    bz = copies(lambda d: (qb.at[x, z],) * 2, zp, every_z)
    start(az)
    start(bz)

    expand[...] = mm_nt(onehot(iota((tok, tok), 0) == iota((tok, tok), 1)), pick).astype(BF)
    lane, col = iota((HD, half), 0), iota((HD, half), 1)
    sel[...] = onehot(((lane & 7) == (col >> log2(HD))) & (lane < 24))

    for c in loads[2:]:
        c.wait()
    ay = copies(lambda d: (qa.at[y],) * 2, yp, every_y)
    bx = copies(lambda d: (qb.at[x],) * 2, xp, every_x)
    ka2 = relay(lambda i, part: ka.at[i, parts[part]], xp, X, x)
    va2 = relay(lambda i, part: va.at[i, parts[part]], xp, X, x)
    kb2 = relay(lambda i, part: kb.at[i, parts[part]], yp, Y, y)
    vb2 = relay(lambda i, part: vb.at[i, parts[part]], yp, Y, y)
    arrive(az)
    start(ay)
    arrive(bz)
    start(bx)
    start(va1[1])
    start(vb1[1])
    arrive(ka1[0])
    start(ka2)
    arrive(kb1[0])
    start(kb2)
    arrive(va1[0])
    start(va2)
    arrive(vb1[0])
    start(vb2)
    arrive(ka1[1])
    arrive(va1[1])

    cut = [pl.ds(0, 48), pl.ds(48, wc - 48)]
    wy0 = copies(lambda d: (wt.at[y, x, :, lo],) * 2, yp, every_y)
    wx1 = copies(lambda d: (wt.at[y, x, :, hi],) * 2, xp, every_x)
    wx0 = copies(lambda d: (wt.at[:, x, :, lo],) * 2, xp, near(X))
    wy1 = copies(lambda d: (wt.at[y, :, :, hi],) * 2, yp, near(Y))
    wx0 = [wx0, relay(lambda i, part: wt.at[:, i, cut[part], lo], xp, X, x)]
    wy1 = [wy1, relay(lambda i, part: wt.at[i, :, cut[part], hi], yp, Y, y)]

    scale = 1.0 / (HD**0.5 * math.log(2.0))
    ones = jnp.ones((tok, HD), BF)
    group = Z * CAP

    def attend(heads, rows, k, v, blocks, sums, peaks, dest, first, last):
        lines = rows.shape[0]
        plane = lines * group
        lane = iota((plane, HD), 1)
        tile = jnp.zeros((plane, HD), F32)
        for i in range(heads):
            c = slice(i * HD, (i + 1) * HD)
            query = rows[:, :, :, c].reshape(plane, HD)
            scores = [mm_nt(query, k[b, :, c]) * scale for b in blocks]
            peak = jnp.max(scores[0], axis=1, keepdims=True)
            for score in scores[1:]:
                peak = jnp.maximum(peak, jnp.max(score, axis=1, keepdims=True))
            if not first:
                old = peaks[i]
                peak = jnp.maximum(old, peak)
            both = None
            for b, score in zip(blocks, scores):
                expo = lax.exp2(score - peak[:, 0:1]).astype(BF)
                part = mm(expo, jnp.concatenate([v[b, :, c], ones], axis=1))
                both = part if both is None else both + part
            if not first:
                fade = lax.exp2(old - peak)
                both = both + sums[i] * jnp.concatenate([fade, fade], axis=1)
            if last:
                total = both[:, HD:]
                dest[:, :, :, c] = (both[:, :HD] / total).astype(BF).reshape(lines, Z, CAP, HD)
                tile = jnp.where((lane & 7) == i, peak + log2_of(total), tile)
            else:
                sums[i] = both
                peaks[i] = jnp.broadcast_to(peak, (plane, HD))
        if last:
            dest[:, :, :, heads * HD :] = pack_stat(tile).reshape(lines, Z, CAP, HD)

    def near_blocks(at_, n):
        return [at_] + [(at_ - d) & (n - 1) for d in near(n)]

    def far_blocks(at_, n):
        return [(at_ - d) & (n - 1) for d in far(n)]

    arrive(ay)
    attend(NA, qa, ka, va, near_blocks(x, X), sum_a, peak_a, pa, True, X <= 3)
    arrive(bx)
    arrive(kb1[1])
    arrive(vb1[1])
    attend(NB, qb, kb, vb, near_blocks(y, Y), sum_b, peak_b, pb, True, Y <= 3)
    start(wy0)
    start(wx1)
    arrive(ka2)
    arrive(va2)
    if X > 3:
        attend(NA, qa, ka, va, far_blocks(x, X), sum_a, peak_a, pa, False, True)
    sa = copies(lambda d: (pa.at[(y + d) & (Y - 1)], ra.at[d - 1]), yp, every_y)
    start(sa)
    arrive(kb2)
    arrive(vb2)
    if Y > 3:
        attend(NB, qb, kb, vb, far_blocks(y, Y), sum_b, peak_b, pb, False, True)
    sb = copies(lambda d: (pb.at[(x + d) & (X - 1)], rb.at[d - 1]), xp, every_x)
    start(sb)
    live = mm(expand[...], jnp.ones((CAP, feat), BF)) > 0.5
    base[...] = jnp.where(live, hid_ref[...].astype(F32), cac_ref[...].astype(F32)).astype(BF)
    pieces = X * Y // H
    extra = pieces * wc - HD
    l, c = iota((2 * HD, feat), 0), iota((2 * HD, feat), 1)
    piece = jnp.where(l < HD, l, l - z * extra)
    mine = (l < HD) | ((l >= HD + z * extra) & (l < HD + (z + 1) * extra))
    goal = jnp.where(piece >= wc, (Z - 1) * wc, 0) + piece
    for d in range(Z):
        places[d] = onehot((goal + ((z - d) & (Z - 1)) * wc == c) & mine)

    arrive(sa)
    arrive(wx1)
    start(wy1[0])

    def merge_in(dest, sources, heads):
        mean, logs = merge([r.reshape(group, r.shape[-1]) for r in sources], heads, sel[...])
        dest[:, :, : heads * HD] = mean.astype(BF).reshape(Z, CAP, heads * HD)
        dest[:, :, heads * HD :] = stat_of(logs, heads).reshape(Z, CAP, HD)

    merge_in(a2, [pa[y]] + [ra[d] for d in range(Y - 1)], NA)
    sa2 = copies(lambda d: (a2.at[(z + d) & (Z - 1)], ra2.at[d - 1]), zp, every_z)
    start(sa2)
    arrive(sb)
    arrive(wy0)
    start(wx0[0])

    merge_in(b2, [pb[x]] + [rb[d] for d in range(X - 1)], NB)
    sb2 = copies(lambda d: (b2.at[(z + d) & (Z - 1)], rb2.at[d - 1]), zp, every_z)
    start(sb2)
    arrive(sa2)
    at[z, :, :half] = merge([a2[z]] + [ra2[d] for d in range(Z - 1)], NA, sel[...])[0].astype(BF)
    tza = copies(lambda d: (at.at[z, :, lo],) * 2, zp, every_z)
    start(tza)
    arrive(wy1[0])
    start(wy1[1])
    arrive(wx0[0])
    start(wx0[1])
    arrive(sb2)
    at[z, :, half:] = merge([b2[z]] + [rb2[d] for d in range(Z - 1)], NB, sel[...])[0].astype(BF)
    tzb = copies(lambda d: (at.at[z, :, hi],) * 2, zp, every_z)
    start(tzb)
    arrive(tza)
    arrive(wx0[1])
    arrive(wy1[1])
    arrive(tzb)

    attn = at[...].reshape(group, feat)
    row, core, chips = h >> 1, h & 1, H // 2

    def terms(which, j):
        at_ = (2 * j + which) * pieces
        w_o = wt[at_ >> log2(X), pl.ds(at_ & (X - 1), pieces)].reshape(pieces * wc, feat)
        term = mm_nt(attn, w_o)
        ht[which, j, 0:group] = term[:, :HD].astype(BF)
        for i in range(Z):
            ht[which, j, group:, i * extra : (i + 1) * extra] = term[i * CAP : (i + 1) * CAP, HD:].astype(BF)

    order = [(row + d) & (chips - 1) for d in [*every_h, 0]]
    sc = []
    for j in order:
        terms(1 - core, j)
        sc.append(copies(lambda d: (ht.at[1 - core, j], hc.at[j]), cp, [1]))
        start(sc[-1])
    for j in order:
        terms(core, j)
    sh = []
    for d, j, c in zip([*every_h, 0], order, sc):
        arrive(c)
        both = ht[core, j].astype(F32) + hc[j].astype(F32)
        if d:
            hs[j] = both.astype(BF)
            sh.append(copies(lambda _: (hs.at[j], hr.at[d - 1]), hp, [d]))
            start(sh[-1])
        else:
            proj = both
    for d in every_h:
        arrive(sh[d - 1])
        proj = proj + hr[d - 1].astype(F32)
    lane = iota((CAP, HD), 1)
    for i in range(Z):
        zs[i, :, :HD] = proj[i * CAP : (i + 1) * CAP].astype(BF)
        zs[i, :, HD:] = jnp.where((lane >= i * extra) & (lane < (i + 1) * extra), proj[group:], 0.0).astype(BF)

    sz = copies(lambda d: (zs.at[(z + d) & (Z - 1)], zr.at[d - 1]), zp, every_z)
    start(sz)

    rows = mm(zs[z], places[0])
    for d in every_z:
        arrive(sz[d - 1 : d])
        rows = rows + mm(zr[d - 1], places[d])
    out_ref[...] = (base[...].astype(F32) + mm(expand[...], rows.astype(BF))).astype(BF)
    for c in every:
        c.wait_send()


def shards(queries, keys, values, hidden, cached, active, w_out):
    tok, feat = queries.shape
    wc = w_out.shape[1]
    fa, fb = NA * HD, NB * HD
    wa, wb = fa + HD, fb + HD
    group = Z * CAP
    n_copies = 120
    vmem = pltpu.VMEM
    scratch = [
        vmem((tok, feat), BF),
        vmem((tok, feat), BF),
        vmem((tok, feat), BF),
        vmem((1, tok), jnp.int32),
        vmem((X, tok, fa), BF),
        vmem((X, tok, fa), BF),
        vmem((Y, tok, fb), BF),
        vmem((Y, tok, fb), BF),
        vmem((Y, Z, CAP, fa), BF),
        vmem((X, Z, CAP, fb), BF),
        vmem((Y, X, wc, feat), BF),
        vmem((HD, fa), BF),
        vmem((tok, CAP), BF),
        vmem((NA, Y * group, 2 * HD), F32),
        vmem((NA, Y * group, HD), F32),
        vmem((NB, X * group, 2 * HD), F32),
        vmem((NB, X * group, HD), F32),
        vmem((Y, Z, CAP, wa), BF),
        vmem((X, Z, CAP, wb), BF),
        vmem((max(Y - 1, 1), Z, CAP, wa), BF),
        vmem((max(X - 1, 1), Z, CAP, wb), BF),
        vmem((Z, CAP, wa), BF),
        vmem((Z, CAP, wb), BF),
        vmem((Z - 1, CAP, wa), BF),
        vmem((Z - 1, CAP, wb), BF),
        vmem((Z, CAP, feat), BF),
        vmem((2, H // 2, group + CAP, HD), BF),
        vmem((H // 2, group + CAP, HD), BF),
        vmem((H // 2, group + CAP, HD), BF),
        vmem((max(H // 2 - 1, 1), group + CAP, HD), BF),
        vmem((Z, CAP, 2 * HD), BF),
        vmem((Z - 1, CAP, 2 * HD), BF),
        vmem((tok, feat), BF),
        vmem((Z, 2 * HD, feat), BF),
        pltpu.SemaphoreType.DMA((n_copies,)),
        pltpu.SemaphoreType.DMA((n_copies,)),
        pltpu.SemaphoreType.DMA((9,)),
    ]
    return pl.pallas_call(
        body,
        out_shape=jax.ShapeDtypeStruct((tok, feat), BF),
        in_specs=[pl.BlockSpec(memory_space=pl.ANY)] * 7,
        out_specs=pl.BlockSpec(memory_space=pltpu.VMEM),
        scratch_shapes=scratch,
        compiler_params=pltpu.CompilerParams(
            collective_id=0, has_side_effects=True, vmem_limit_bytes=60 * 2**20
        ),
    )(queries, keys, values, hidden, cached, active.reshape(1, tok), w_out.T)


def solution(mesh):
    placed = (
        P("seq", "head"),
        P("seq", "head"),
        P("seq", "head"),
        P("seq", "head"),
        P("seq", "head"),
        P("seq"),
        P("head", "seq"),
    )
    return jax.shard_map(
        shards, mesh=mesh, in_specs=placed, out_specs=P("seq", "head"), check_vma=False
    )
```

```python
import math

import jax
import jax.numpy as jnp
from jax import lax
from jax.experimental import pallas as pl
from jax.experimental.pallas import tpu as pltpu
from jax.sharding import PartitionSpec as P

X, Y, Z, H = 4, 4, 4, 8
HD = 128
CAP = 32
BF = jnp.bfloat16
F32 = jnp.float32
NA, NB = 3, 2
MESH = pl.DeviceIdType.MESH


def log2(n):
    return n.bit_length() - 1


def iota(shape, dim):
    return lax.broadcasted_iota(jnp.int32, shape, dim)


def onehot(cond):
    return jnp.where(cond, 1.0, 0.0).astype(BF)


def log2_of(v):
    return jnp.log(v) * (1.0 / math.log(2.0))


def mm(a, b):
    return jnp.dot(a, b, preferred_element_type=F32)


def mm_nt(a, b):
    return lax.dot_general(a, b, (((1,), (1,)), ((), ())), preferred_element_type=F32)


def pack_stat(tile):
    lane = iota(tile.shape, 1)
    hi = tile.astype(BF).astype(F32)
    rest = tile - hi
    mid = rest.astype(BF).astype(F32)
    low = rest - mid
    return jnp.where(lane < 8, hi, jnp.where(lane < 16, mid, jnp.where(lane < 24, low, 0.0))).astype(BF)


def merge(sources, heads, sel):
    width = heads * HD
    logs = [mm(s[:, width:], sel[:, :width]) for s in sources]
    top = logs[0]
    for part in logs[1:]:
        top = jnp.maximum(top, part)
    total, mixed = None, None
    for s, part in zip(sources, logs):
        w = lax.exp2(part - top)
        term = w * s[:, :width].astype(F32)
        total = w if total is None else total + w
        mixed = term if mixed is None else mixed + term
    return mixed / total, top + log2_of(total)


def stat_of(logs, heads):
    lane = iota((logs.shape[0], HD), 1)
    tile = jnp.zeros((logs.shape[0], HD), F32)
    for h in range(heads):
        tile = jnp.where((lane & 7) == h, logs[:, h * HD : (h + 1) * HD], tile)
    return pack_stat(tile)


def body(
    q_hbm, k_hbm, v_hbm, hid_hbm, cac_hbm, act_hbm, w_hbm, out_ref,
    q_ref, hid_ref, cac_ref, act_ref,
    ka, va, kb, vb, qa, qb, wt, sel, expand,
    sum_a, peak_a, sum_b, peak_b,
    pa, pb, ra, rb, a2, b2, ra2, rb2, at,
    ht, hc, hs, hr, zs, zr, base, places, send_sem, recv_sem, load_sem,
):
    tok, feat = q_ref.shape
    wc = w_hbm.shape[0]
    half = NA * HD
    me, h = lax.axis_index("seq"), lax.axis_index("head")
    z = me & (Z - 1)
    x = (me >> log2(Z)) & (X - 1)
    y = me >> log2(Z * X)

    def xp(d):
        return (y * X + ((x + d) & (X - 1))) * Z + z, h

    def yp(d):
        return (((y + d) & (Y - 1)) * X + x) * Z + z, h

    def zp(d):
        return (y * X + x) * Z + ((z + d) & (Z - 1)), h

    def cp(d):
        return me, h ^ 1

    def hp(d):
        return me, (((h >> 1) + d) & (H // 2 - 1)) * 2 + (h & 1)

    barrier = pltpu.get_barrier_semaphore()
    peers = (
        [xp(d) for d in range(1, X)] + [yp(d) for d in range(1, Y)] + [zp(d) for d in range(1, Z)] + [hp(d) for d in range(1, H // 2)] + [cp(1)]
    )
    for p in peers:
        pl.semaphore_signal(barrier, inc=1, device_id=p, device_id_type=MESH)

    lo, hi = pl.ds(0, half), pl.ds(half, feat - half)
    loads = [
        pltpu.make_async_copy(src, dst, load_sem.at[i])
        for i, (src, dst) in enumerate(
            [
                (act_hbm, act_ref), (q_hbm, q_ref),
                (k_hbm.at[:, lo], ka.at[x]), (k_hbm.at[:, hi], kb.at[y]),
                (v_hbm.at[:, lo], va.at[x]), (v_hbm.at[:, hi], vb.at[y]),
                (w_hbm, wt.at[y, x]), (hid_hbm, hid_ref), (cac_hbm, cac_ref),
            ]
        )
    ]
    for c in loads:
        c.start()

    counter = [0]
    every = []

    def copies(make, peer, steps):
        found = []
        for d in steps:
            i = counter[0]
            counter[0] += 1
            src, dst = make(d)
            found.append(
                pltpu.make_async_remote_copy(
                    src_ref=src, dst_ref=dst, send_sem=send_sem.at[i], recv_sem=recv_sem.at[i],
                    device_id=peer(d), device_id_type=MESH,
                )
            )
        return found

    def start(cs):
        for c in cs:
            c.start()
        every.extend(cs)

    def arrive(cs):
        for c in cs:
            c.wait_recv()

    def near(n):
        return [1, n - 1] if n > 2 else list(range(1, n))

    def far(n):
        return list(range(2, n - 1))

    def relay(block, peer, n, at_):
        if n <= 3:
            return []
        on = copies(lambda d: (block((at_ - 1) & (n - 1), 0),) * 2, peer, [1])
        return on + copies(lambda d: (block((at_ + 1) & (n - 1), 1),) * 2, peer, [n - 1])

    every_x, every_y, every_z, every_h = range(1, X), range(1, Y), range(1, Z), range(1, H // 2)

    pl.semaphore_wait(barrier, len(peers))

    parts = [pl.ds(0, tok // 2), pl.ds(tok // 2, tok // 2)]

    def near_copies(src, cols, dst, at_, peer, n, second):
        found = []
        for d in near(n):
            rows = parts[int(d != 1) ^ second]
            found += copies(lambda _: (src.at[rows, cols], dst.at[at_, rows]), peer, [d])
        return found

    ka1, va1, kb1, vb1 = ([
        near_copies(src, cols, dst, at_, peer, n, second) for second in (0, 1)
    ] for src, cols, dst, at_, peer, n in (
        (k_hbm, lo, ka, x, xp, X), (v_hbm, lo, va, x, xp, X), (k_hbm, hi, kb, y, yp, Y), (v_hbm, hi, vb, y, yp, Y),
    ))
    for c in (ka1[0], kb1[0], va1[0], vb1[0], ka1[1], kb1[1]):
        start(c)

    loads[0].wait()
    act = act_ref[...]
    act8 = jnp.broadcast_to(act, (8, tok)).astype(F32).astype(BF)
    before = onehot(iota((tok, tok), 0) < iota((tok, tok), 1))
    rank = mm(act8, before)[0:1, :]
    pick = onehot((iota((CAP, tok), 0).astype(F32) == rank) & (act > 0))
    loads[1].wait()
    own = mm(pick, q_ref[...]).astype(BF)
    qa[y, z] = own[:, :half]
    qb[x, z] = own[:, half:]
    az = copies(lambda d: (qa.at[y, z],) * 2, zp, every_z)
    bz = copies(lambda d: (qb.at[x, z],) * 2, zp, every_z)
    start(az)
    start(bz)

    expand[...] = mm_nt(onehot(iota((tok, tok), 0) == iota((tok, tok), 1)), pick).astype(BF)
    lane, col = iota((HD, half), 0), iota((HD, half), 1)
    sel[...] = onehot(((lane & 7) == (col >> log2(HD))) & (lane < 24))

    for c in loads[2:]:
        c.wait()
    ay = copies(lambda d: (qa.at[y],) * 2, yp, every_y)
    bx = copies(lambda d: (qb.at[x],) * 2, xp, every_x)
    ka2 = relay(lambda i, part: ka.at[i, parts[part]], xp, X, x)
    va2 = relay(lambda i, part: va.at[i, parts[part]], xp, X, x)
    kb2 = relay(lambda i, part: kb.at[i, parts[part]], yp, Y, y)
    vb2 = relay(lambda i, part: vb.at[i, parts[part]], yp, Y, y)
    arrive(az)
    start(ay)
    arrive(bz)
    start(bx)
    start(va1[1])
    start(vb1[1])
    arrive(ka1[0])
    start(ka2)
    arrive(kb1[0])
    start(kb2)
    arrive(va1[0])
    start(va2)
    arrive(vb1[0])
    start(vb2)
    arrive(ka1[1])
    arrive(va1[1])

    cut = [pl.ds(0, 48), pl.ds(48, wc - 48)]
    wy0 = copies(lambda d: (wt.at[y, x, :, lo],) * 2, yp, every_y)
    wx1 = copies(lambda d: (wt.at[y, x, :, hi],) * 2, xp, every_x)
    wx0 = copies(lambda d: (wt.at[:, x, :, lo],) * 2, xp, near(X))
    wy1 = copies(lambda d: (wt.at[y, :, :, hi],) * 2, yp, near(Y))
    wx0 = [wx0, relay(lambda i, part: wt.at[:, i, cut[part], lo], xp, X, x)]
    wy1 = [wy1, relay(lambda i, part: wt.at[i, :, cut[part], hi], yp, Y, y)]

    scale = 1.0 / (HD**0.5 * math.log(2.0))
    ones = jnp.ones((tok, HD), BF)
    group = Z * CAP

    def attend(heads, rows, k, v, blocks, sums, peaks, dest, first, last):
        lines = rows.shape[0]
        plane = lines * group
        lane = iota((plane, HD), 1)
        tile = jnp.zeros((plane, HD), F32)
        for i in range(heads):
            c = slice(i * HD, (i + 1) * HD)
            query = rows[:, :, :, c].reshape(plane, HD)
            scores = [mm_nt(query, k[b, :, c]) * scale for b in blocks]
            peak = jnp.max(scores[0], axis=1, keepdims=True)
            for score in scores[1:]:
                peak = jnp.maximum(peak, jnp.max(score, axis=1, keepdims=True))
            if not first:
                old = peaks[i]
                peak = jnp.maximum(old, peak)
            both = None
            for b, score in zip(blocks, scores):
                expo = lax.exp2(score - peak[:, 0:1]).astype(BF)
                part = mm(expo, jnp.concatenate([v[b, :, c], ones], axis=1))
                both = part if both is None else both + part
            if not first:
                fade = lax.exp2(old - peak)
                both = both + sums[i] * jnp.concatenate([fade, fade], axis=1)
            if last:
                total = both[:, HD:]
                dest[:, :, :, c] = (both[:, :HD] / total).astype(BF).reshape(lines, Z, CAP, HD)
                tile = jnp.where((lane & 7) == i, peak + log2_of(total), tile)
            else:
                sums[i] = both
                peaks[i] = jnp.broadcast_to(peak, (plane, HD))
        if last:
            dest[:, :, :, heads * HD :] = pack_stat(tile).reshape(lines, Z, CAP, HD)

    def near_blocks(at_, n):
        return [at_] + [(at_ - d) & (n - 1) for d in near(n)]

    def far_blocks(at_, n):
        return [(at_ - d) & (n - 1) for d in far(n)]

    start(wy0)
    start(wx1)
    arrive(ay)
    attend(NA, qa, ka, va, near_blocks(x, X), sum_a, peak_a, pa, True, X <= 3)
    arrive(bx)
    arrive(kb1[1])
    arrive(vb1[1])
    attend(NB, qb, kb, vb, near_blocks(y, Y), sum_b, peak_b, pb, True, Y <= 3)
    arrive(ka2)
    arrive(va2)
    if X > 3:
        attend(NA, qa, ka, va, far_blocks(x, X), sum_a, peak_a, pa, False, True)
    sa = copies(lambda d: (pa.at[(y + d) & (Y - 1)], ra.at[d - 1]), yp, every_y)
    start(sa)
    arrive(kb2)
    arrive(vb2)
    if Y > 3:
        attend(NB, qb, kb, vb, far_blocks(y, Y), sum_b, peak_b, pb, False, True)
    sb = copies(lambda d: (pb.at[(x + d) & (X - 1)], rb.at[d - 1]), xp, every_x)
    start(sb)
    live = mm(expand[...], jnp.ones((CAP, feat), BF)) > 0.5
    base[...] = jnp.where(live, hid_ref[...].astype(F32), cac_ref[...].astype(F32)).astype(BF)
    pieces = X * Y // H
    extra = pieces * wc - HD
    l, c = iota((2 * HD, feat), 0), iota((2 * HD, feat), 1)
    piece = jnp.where(l < HD, l, l - z * extra)
    mine = (l < HD) | ((l >= HD + z * extra) & (l < HD + (z + 1) * extra))
    goal = jnp.where(piece >= wc, (Z - 1) * wc, 0) + piece
    for d in range(Z):
        places[d] = onehot((goal + ((z - d) & (Z - 1)) * wc == c) & mine)

    arrive(sa)
    arrive(wx1)
    start(wy1[0])

    def merge_in(dest, sources, heads):
        mean, logs = merge([r.reshape(group, r.shape[-1]) for r in sources], heads, sel[...])
        dest[:, :, : heads * HD] = mean.astype(BF).reshape(Z, CAP, heads * HD)
        dest[:, :, heads * HD :] = stat_of(logs, heads).reshape(Z, CAP, HD)

    merge_in(a2, [pa[y]] + [ra[d] for d in range(Y - 1)], NA)
    sa2 = copies(lambda d: (a2.at[(z + d) & (Z - 1)], ra2.at[d - 1]), zp, every_z)
    start(sa2)
    arrive(sb)
    arrive(wy0)
    start(wx0[0])

    merge_in(b2, [pb[x]] + [rb[d] for d in range(X - 1)], NB)
    sb2 = copies(lambda d: (b2.at[(z + d) & (Z - 1)], rb2.at[d - 1]), zp, every_z)
    start(sb2)
    arrive(sa2)
    at[z, :, :half] = merge([a2[z]] + [ra2[d] for d in range(Z - 1)], NA, sel[...])[0].astype(BF)
    tza = copies(lambda d: (at.at[z, :, lo],) * 2, zp, every_z)
    start(tza)
    arrive(wy1[0])
    start(wy1[1])
    arrive(wx0[0])
    start(wx0[1])
    arrive(sb2)
    at[z, :, half:] = merge([b2[z]] + [rb2[d] for d in range(Z - 1)], NB, sel[...])[0].astype(BF)
    tzb = copies(lambda d: (at.at[z, :, hi],) * 2, zp, every_z)
    start(tzb)
    arrive(tza)
    arrive(wx0[1])
    arrive(wy1[1])
    arrive(tzb)

    attn = at[...].reshape(group, feat)
    row, core, chips = h >> 1, h & 1, H // 2

    def terms(which, j):
        at_ = (2 * j + which) * pieces
        w_o = wt[at_ >> log2(X), pl.ds(at_ & (X - 1), pieces)].reshape(pieces * wc, feat)
        term = mm_nt(attn, w_o)
        ht[which, j, 0:group] = term[:, :HD].astype(BF)
        for i in range(Z):
            ht[which, j, group:, i * extra : (i + 1) * extra] = term[i * CAP : (i + 1) * CAP, HD:].astype(BF)

    order = [(row + d) & (chips - 1) for d in [*every_h, 0]]
    sc = []
    for j in order:
        terms(1 - core, j)
        sc.append(copies(lambda d: (ht.at[1 - core, j], hc.at[j]), cp, [1]))
        start(sc[-1])
    for j in order:
        terms(core, j)
    sh = []
    for d, j, c in zip([*every_h, 0], order, sc):
        arrive(c)
        both = ht[core, j].astype(F32) + hc[j].astype(F32)
        if d:
            hs[j] = both.astype(BF)
            sh.append(copies(lambda _: (hs.at[j], hr.at[d - 1]), hp, [d]))
            start(sh[-1])
        else:
            proj = both
    for d in every_h:
        arrive(sh[d - 1])
        proj = proj + hr[d - 1].astype(F32)
    lane = iota((CAP, HD), 1)
    for i in range(Z):
        zs[i, :, :HD] = proj[i * CAP : (i + 1) * CAP].astype(BF)
        zs[i, :, HD:] = jnp.where((lane >= i * extra) & (lane < (i + 1) * extra), proj[group:], 0.0).astype(BF)

    sz = copies(lambda d: (zs.at[(z + d) & (Z - 1)], zr.at[d - 1]), zp, every_z)
    start(sz)

    rows = mm(zs[z], places[0])
    for d in every_z:
        arrive(sz[d - 1 : d])
        rows = rows + mm(zr[d - 1], places[d])
    out_ref[...] = (base[...].astype(F32) + mm(expand[...], rows.astype(BF))).astype(BF)
    for c in every:
        c.wait_send()


def shards(queries, keys, values, hidden, cached, active, w_out):
    tok, feat = queries.shape
    wc = w_out.shape[1]
    fa, fb = NA * HD, NB * HD
    wa, wb = fa + HD, fb + HD
    group = Z * CAP
    n_copies = 120
    vmem = pltpu.VMEM
    scratch = [
        vmem((tok, feat), BF),
        vmem((tok, feat), BF),
        vmem((tok, feat), BF),
        vmem((1, tok), jnp.int32),
        vmem((X, tok, fa), BF),
        vmem((X, tok, fa), BF),
        vmem((Y, tok, fb), BF),
        vmem((Y, tok, fb), BF),
        vmem((Y, Z, CAP, fa), BF),
        vmem((X, Z, CAP, fb), BF),
        vmem((Y, X, wc, feat), BF),
        vmem((HD, fa), BF),
        vmem((tok, CAP), BF),
        vmem((NA, Y * group, 2 * HD), F32),
        vmem((NA, Y * group, HD), F32),
        vmem((NB, X * group, 2 * HD), F32),
        vmem((NB, X * group, HD), F32),
        vmem((Y, Z, CAP, wa), BF),
        vmem((X, Z, CAP, wb), BF),
        vmem((max(Y - 1, 1), Z, CAP, wa), BF),
        vmem((max(X - 1, 1), Z, CAP, wb), BF),
        vmem((Z, CAP, wa), BF),
        vmem((Z, CAP, wb), BF),
        vmem((Z - 1, CAP, wa), BF),
        vmem((Z - 1, CAP, wb), BF),
        vmem((Z, CAP, feat), BF),
        vmem((2, H // 2, group + CAP, HD), BF),
        vmem((H // 2, group + CAP, HD), BF),
        vmem((H // 2, group + CAP, HD), BF),
        vmem((max(H // 2 - 1, 1), group + CAP, HD), BF),
        vmem((Z, CAP, 2 * HD), BF),
        vmem((Z - 1, CAP, 2 * HD), BF),
        vmem((tok, feat), BF),
        vmem((Z, 2 * HD, feat), BF),
        pltpu.SemaphoreType.DMA((n_copies,)),
        pltpu.SemaphoreType.DMA((n_copies,)),
        pltpu.SemaphoreType.DMA((9,)),
    ]
    return pl.pallas_call(
        body,
        out_shape=jax.ShapeDtypeStruct((tok, feat), BF),
        in_specs=[pl.BlockSpec(memory_space=pl.ANY)] * 7,
        out_specs=pl.BlockSpec(memory_space=pltpu.VMEM),
        scratch_shapes=scratch,
        compiler_params=pltpu.CompilerParams(
            collective_id=0, has_side_effects=True, vmem_limit_bytes=60 * 2**20
        ),
    )(queries, keys, values, hidden, cached, active.reshape(1, tok), w_out.T)


def solution(mesh):
    placed = (
        P("seq", "head"),
        P("seq", "head"),
        P("seq", "head"),
        P("seq", "head"),
        P("seq", "head"),
        P("seq"),
        P("head", "seq"),
    )
    return jax.shard_map(
        shards, mesh=mesh, in_specs=placed, out_specs=P("seq", "head"), check_vma=False
    )
```

```python
import math

import jax
import jax.numpy as jnp
from jax import lax
from jax.experimental import pallas as pl
from jax.experimental.pallas import tpu as pltpu
from jax.sharding import PartitionSpec as P

X, Y, Z, H = 4, 4, 4, 8
HD = 128
CAP = 32
BF = jnp.bfloat16
F32 = jnp.float32
NA, NB = 3, 2
MESH = pl.DeviceIdType.MESH


def log2(n):
    return n.bit_length() - 1


def iota(shape, dim):
    return lax.broadcasted_iota(jnp.int32, shape, dim)


def onehot(cond):
    return jnp.where(cond, 1.0, 0.0).astype(BF)


def log2_of(v):
    return jnp.log(v) * (1.0 / math.log(2.0))


def mm(a, b):
    return jnp.dot(a, b, preferred_element_type=F32)


def mm_nt(a, b):
    return lax.dot_general(a, b, (((1,), (1,)), ((), ())), preferred_element_type=F32)


def pack_stat(tile):
    lane = iota(tile.shape, 1)
    hi = tile.astype(BF).astype(F32)
    rest = tile - hi
    mid = rest.astype(BF).astype(F32)
    low = rest - mid
    return jnp.where(lane < 8, hi, jnp.where(lane < 16, mid, jnp.where(lane < 24, low, 0.0))).astype(BF)


def merge(sources, heads, sel):
    width = heads * HD
    logs = [mm(s[:, width:], sel[:, :width]) for s in sources]
    top = logs[0]
    for part in logs[1:]:
        top = jnp.maximum(top, part)
    total, mixed = None, None
    for s, part in zip(sources, logs):
        w = lax.exp2(part - top)
        term = w * s[:, :width].astype(F32)
        total = w if total is None else total + w
        mixed = term if mixed is None else mixed + term
    return mixed / total, top + log2_of(total)


def stat_of(logs, heads):
    lane = iota((logs.shape[0], HD), 1)
    tile = jnp.zeros((logs.shape[0], HD), F32)
    for h in range(heads):
        tile = jnp.where((lane & 7) == h, logs[:, h * HD : (h + 1) * HD], tile)
    return pack_stat(tile)


def body(
    q_hbm, k_hbm, v_hbm, hid_hbm, cac_hbm, act_hbm, w_hbm, out_ref,
    q_ref, hid_ref, cac_ref, act_ref,
    ka, va, kb, vb, qa, qb, wt, sel, expand,
    sum_a, peak_a, sum_b, peak_b,
    pa, pb, ra, rb, a2, b2, ra2, rb2, at,
    ht, hc, hs, hr, zs, zr, base, places, send_sem, recv_sem, load_sem,
):
    tok, feat = q_ref.shape
    wc = w_hbm.shape[0]
    half = NA * HD
    me, h = lax.axis_index("seq"), lax.axis_index("head")
    z = me & (Z - 1)
    x = (me >> log2(Z)) & (X - 1)
    y = me >> log2(Z * X)

    def xp(d):
        return (y * X + ((x + d) & (X - 1))) * Z + z, h

    def yp(d):
        return (((y + d) & (Y - 1)) * X + x) * Z + z, h

    def zp(d):
        return (y * X + x) * Z + ((z + d) & (Z - 1)), h

    def cp(d):
        return me, h ^ 1

    def hp(d):
        return me, (((h >> 1) + d) & (H // 2 - 1)) * 2 + (h & 1)

    barrier = pltpu.get_barrier_semaphore()
    peers = (
        [xp(d) for d in range(1, X)] + [yp(d) for d in range(1, Y)] + [zp(d) for d in range(1, Z)] + [hp(d) for d in range(1, H // 2)] + [cp(1)]
    )
    for p in peers:
        pl.semaphore_signal(barrier, inc=1, device_id=p, device_id_type=MESH)

    lo, hi = pl.ds(0, half), pl.ds(half, feat - half)
    loads = [
        pltpu.make_async_copy(src, dst, load_sem.at[i])
        for i, (src, dst) in enumerate(
            [
                (act_hbm, act_ref), (q_hbm, q_ref),
                (k_hbm.at[:, lo], ka.at[x]), (k_hbm.at[:, hi], kb.at[y]),
                (v_hbm.at[:, lo], va.at[x]), (v_hbm.at[:, hi], vb.at[y]),
                (w_hbm, wt.at[y, x]), (hid_hbm, hid_ref), (cac_hbm, cac_ref),
            ]
        )
    ]
    for c in loads:
        c.start()

    counter = [0]
    every = []

    def copies(make, peer, steps):
        found = []
        for d in steps:
            i = counter[0]
            counter[0] += 1
            src, dst = make(d)
            found.append(
                pltpu.make_async_remote_copy(
                    src_ref=src, dst_ref=dst, send_sem=send_sem.at[i], recv_sem=recv_sem.at[i],
                    device_id=peer(d), device_id_type=MESH,
                )
            )
        return found

    def start(cs):
        for c in cs:
            c.start()
        every.extend(cs)

    def arrive(cs):
        for c in cs:
            c.wait_recv()

    def near(n):
        return [1, n - 1] if n > 2 else list(range(1, n))

    def far(n):
        return list(range(2, n - 1))

    def relay(block, peer, n, at_):
        if n <= 3:
            return []
        on = copies(lambda d: (block((at_ - 1) & (n - 1), 0),) * 2, peer, [1])
        return on + copies(lambda d: (block((at_ + 1) & (n - 1), 1),) * 2, peer, [n - 1])

    every_x, every_y, every_z, every_h = range(1, X), range(1, Y), range(1, Z), range(1, H // 2)

    pl.semaphore_wait(barrier, len(peers))

    parts = [pl.ds(0, tok // 2), pl.ds(tok // 2, tok // 2)]

    def near_copies(src, cols, dst, at_, peer, n, second):
        found = []
        for d in near(n):
            rows = parts[int(d != 1) ^ second]
            found += copies(lambda _: (src.at[rows, cols], dst.at[at_, rows]), peer, [d])
        return found

    ka1, va1, kb1, vb1 = ([
        near_copies(src, cols, dst, at_, peer, n, second) for second in (0, 1)
    ] for src, cols, dst, at_, peer, n in (
        (k_hbm, lo, ka, x, xp, X), (v_hbm, lo, va, x, xp, X), (k_hbm, hi, kb, y, yp, Y), (v_hbm, hi, vb, y, yp, Y),
    ))
    for c in (ka1[0], kb1[0], va1[0], vb1[0], ka1[1], kb1[1]):
        start(c)

    loads[0].wait()
    act = act_ref[...]
    act8 = jnp.broadcast_to(act, (8, tok)).astype(F32).astype(BF)
    before = onehot(iota((tok, tok), 0) < iota((tok, tok), 1))
    rank = mm(act8, before)[0:1, :]
    pick = onehot((iota((CAP, tok), 0).astype(F32) == rank) & (act > 0))
    loads[1].wait()
    own = mm(pick, q_ref[...]).astype(BF)
    qa[y, z] = own[:, :half]
    qb[x, z] = own[:, half:]
    az = copies(lambda d: (qa.at[y, z],) * 2, zp, every_z)
    bz = copies(lambda d: (qb.at[x, z],) * 2, zp, every_z)
    start(az)
    start(bz)

    expand[...] = mm_nt(onehot(iota((tok, tok), 0) == iota((tok, tok), 1)), pick).astype(BF)
    lane, col = iota((HD, half), 0), iota((HD, half), 1)
    sel[...] = onehot(((lane & 7) == (col >> log2(HD))) & (lane < 24))

    for c in loads[2:]:
        c.wait()
    ay = copies(lambda d: (qa.at[y],) * 2, yp, every_y)
    bx = copies(lambda d: (qb.at[x],) * 2, xp, every_x)
    ka2 = relay(lambda i, part: ka.at[i, parts[part]], xp, X, x)
    va2 = relay(lambda i, part: va.at[i, parts[part]], xp, X, x)
    kb2 = relay(lambda i, part: kb.at[i, parts[part]], yp, Y, y)
    vb2 = relay(lambda i, part: vb.at[i, parts[part]], yp, Y, y)
    arrive(az)
    start(ay)
    arrive(bz)
    start(bx)
    start(va1[1])
    start(vb1[1])
    arrive(ka1[0])
    start(ka2)
    arrive(kb1[0])
    start(kb2)
    arrive(va1[0])
    start(va2)
    arrive(vb1[0])
    start(vb2)
    arrive(ka1[1])
    arrive(va1[1])

    cut = [pl.ds(0, 48), pl.ds(48, wc - 48)]
    wy0 = copies(lambda d: (wt.at[y, x, :, lo],) * 2, yp, every_y)
    wx1 = copies(lambda d: (wt.at[y, x, :, hi],) * 2, xp, every_x)
    wx0 = copies(lambda d: (wt.at[:, x, :, lo],) * 2, xp, near(X))
    wy1 = copies(lambda d: (wt.at[y, :, :, hi],) * 2, yp, near(Y))
    wx0 = [wx0, relay(lambda i, part: wt.at[:, i, cut[part], lo], xp, X, x)]
    wy1 = [wy1, relay(lambda i, part: wt.at[i, :, cut[part], hi], yp, Y, y)]

    scale = 1.0 / (HD**0.5 * math.log(2.0))
    ones = jnp.ones((tok, HD), BF)
    group = Z * CAP

    def attend(heads, rows, k, v, blocks, sums, peaks, dest, first, last):
        lines = rows.shape[0]
        plane = lines * group
        lane = iota((plane, HD), 1)
        tile = jnp.zeros((plane, HD), F32)
        for i in range(heads):
            c = slice(i * HD, (i + 1) * HD)
            query = rows[:, :, :, c].reshape(plane, HD)
            scores = [mm_nt(query, k[b, :, c]) * scale for b in blocks]
            peak = jnp.max(scores[0], axis=1, keepdims=True)
            for score in scores[1:]:
                peak = jnp.maximum(peak, jnp.max(score, axis=1, keepdims=True))
            if not first:
                old = peaks[i]
                peak = jnp.maximum(old, peak)
            both = None
            for b, score in zip(blocks, scores):
                expo = lax.exp2(score - peak[:, 0:1]).astype(BF)
                part = mm(expo, jnp.concatenate([v[b, :, c], ones], axis=1))
                both = part if both is None else both + part
            if not first:
                fade = lax.exp2(old - peak)
                both = both + sums[i] * jnp.concatenate([fade, fade], axis=1)
            if last:
                total = both[:, HD:]
                dest[:, :, :, c] = (both[:, :HD] / total).astype(BF).reshape(lines, Z, CAP, HD)
                tile = jnp.where((lane & 7) == i, peak + log2_of(total), tile)
            else:
                sums[i] = both
                peaks[i] = jnp.broadcast_to(peak, (plane, HD))
        if last:
            dest[:, :, :, heads * HD :] = pack_stat(tile).reshape(lines, Z, CAP, HD)

    def near_blocks(at_, n):
        return [at_] + [(at_ - d) & (n - 1) for d in near(n)]

    def far_blocks(at_, n):
        return [(at_ - d) & (n - 1) for d in far(n)]

    start(wy0)
    start(wx1)
    arrive(ay)
    attend(NA, qa, ka, va, near_blocks(x, X), sum_a, peak_a, pa, True, X <= 3)
    arrive(bx)
    arrive(kb1[1])
    arrive(vb1[1])
    attend(NB, qb, kb, vb, near_blocks(y, Y), sum_b, peak_b, pb, True, Y <= 3)
    arrive(ka2)
    arrive(va2)
    if X > 3:
        attend(NA, qa, ka, va, far_blocks(x, X), sum_a, peak_a, pa, False, True)
    sa = copies(lambda d: (pa.at[(y + d) & (Y - 1)], ra.at[d - 1]), yp, every_y)
    start(sa)
    arrive(kb2)
    arrive(vb2)
    if Y > 3:
        attend(NB, qb, kb, vb, far_blocks(y, Y), sum_b, peak_b, pb, False, True)
    sb = copies(lambda d: (pb.at[(x + d) & (X - 1)], rb.at[d - 1]), xp, every_x)
    start(sb)
    arrive(wx1)
    start(wy1[0])
    arrive(wy0)
    start(wx0[0])
    live = mm(expand[...], jnp.ones((CAP, feat), BF)) > 0.5
    base[...] = jnp.where(live, hid_ref[...].astype(F32), cac_ref[...].astype(F32)).astype(BF)
    pieces = X * Y // H
    extra = pieces * wc - HD
    l, c = iota((2 * HD, feat), 0), iota((2 * HD, feat), 1)
    piece = jnp.where(l < HD, l, l - z * extra)
    mine = (l < HD) | ((l >= HD + z * extra) & (l < HD + (z + 1) * extra))
    goal = jnp.where(piece >= wc, (Z - 1) * wc, 0) + piece
    for d in range(Z):
        places[d] = onehot((goal + ((z - d) & (Z - 1)) * wc == c) & mine)

    arrive(sa)

    def merge_in(dest, sources, heads):
        mean, logs = merge([r.reshape(group, r.shape[-1]) for r in sources], heads, sel[...])
        dest[:, :, : heads * HD] = mean.astype(BF).reshape(Z, CAP, heads * HD)
        dest[:, :, heads * HD :] = stat_of(logs, heads).reshape(Z, CAP, HD)

    merge_in(a2, [pa[y]] + [ra[d] for d in range(Y - 1)], NA)
    sa2 = copies(lambda d: (a2.at[(z + d) & (Z - 1)], ra2.at[d - 1]), zp, every_z)
    start(sa2)
    arrive(sb)

    merge_in(b2, [pb[x]] + [rb[d] for d in range(X - 1)], NB)
    sb2 = copies(lambda d: (b2.at[(z + d) & (Z - 1)], rb2.at[d - 1]), zp, every_z)
    start(sb2)
    arrive(sa2)
    at[z, :, :half] = merge([a2[z]] + [ra2[d] for d in range(Z - 1)], NA, sel[...])[0].astype(BF)
    tza = copies(lambda d: (at.at[z, :, lo],) * 2, zp, every_z)
    start(tza)
    arrive(wy1[0])
    start(wy1[1])
    arrive(wx0[0])
    start(wx0[1])
    arrive(sb2)
    at[z, :, half:] = merge([b2[z]] + [rb2[d] for d in range(Z - 1)], NB, sel[...])[0].astype(BF)
    tzb = copies(lambda d: (at.at[z, :, hi],) * 2, zp, every_z)
    start(tzb)
    arrive(tza)
    arrive(wx0[1])
    arrive(wy1[1])
    arrive(tzb)

    attn = at[...].reshape(group, feat)
    row, core, chips = h >> 1, h & 1, H // 2

    def terms(which, j):
        at_ = (2 * j + which) * pieces
        w_o = wt[at_ >> log2(X), pl.ds(at_ & (X - 1), pieces)].reshape(pieces * wc, feat)
        term = mm_nt(attn, w_o)
        ht[which, j, 0:group] = term[:, :HD].astype(BF)
        for i in range(Z):
            ht[which, j, group:, i * extra : (i + 1) * extra] = term[i * CAP : (i + 1) * CAP, HD:].astype(BF)

    order = [(row + d) & (chips - 1) for d in [*every_h, 0]]
    sc = []
    for j in order:
        terms(1 - core, j)
        sc.append(copies(lambda d: (ht.at[1 - core, j], hc.at[j]), cp, [1]))
        start(sc[-1])
    for j in order:
        terms(core, j)
    sh = []
    for d, j, c in zip([*every_h, 0], order, sc):
        arrive(c)
        both = ht[core, j].astype(F32) + hc[j].astype(F32)
        if d:
            hs[j] = both.astype(BF)
            sh.append(copies(lambda _: (hs.at[j], hr.at[d - 1]), hp, [d]))
            start(sh[-1])
        else:
            proj = both
    for d in every_h:
        arrive(sh[d - 1])
        proj = proj + hr[d - 1].astype(F32)
    lane = iota((CAP, HD), 1)
    for i in range(Z):
        zs[i, :, :HD] = proj[i * CAP : (i + 1) * CAP].astype(BF)
        zs[i, :, HD:] = jnp.where((lane >= i * extra) & (lane < (i + 1) * extra), proj[group:], 0.0).astype(BF)

    sz = copies(lambda d: (zs.at[(z + d) & (Z - 1)], zr.at[d - 1]), zp, every_z)
    start(sz)

    rows = mm(zs[z], places[0])
    for d in every_z:
        arrive(sz[d - 1 : d])
        rows = rows + mm(zr[d - 1], places[d])
    out_ref[...] = (base[...].astype(F32) + mm(expand[...], rows.astype(BF))).astype(BF)
    for c in every:
        c.wait_send()


def shards(queries, keys, values, hidden, cached, active, w_out):
    tok, feat = queries.shape
    wc = w_out.shape[1]
    fa, fb = NA * HD, NB * HD
    wa, wb = fa + HD, fb + HD
    group = Z * CAP
    n_copies = 120
    vmem = pltpu.VMEM
    scratch = [
        vmem((tok, feat), BF),
        vmem((tok, feat), BF),
        vmem((tok, feat), BF),
        vmem((1, tok), jnp.int32),
        vmem((X, tok, fa), BF),
        vmem((X, tok, fa), BF),
        vmem((Y, tok, fb), BF),
        vmem((Y, tok, fb), BF),
        vmem((Y, Z, CAP, fa), BF),
        vmem((X, Z, CAP, fb), BF),
        vmem((Y, X, wc, feat), BF),
        vmem((HD, fa), BF),
        vmem((tok, CAP), BF),
        vmem((NA, Y * group, 2 * HD), F32),
        vmem((NA, Y * group, HD), F32),
        vmem((NB, X * group, 2 * HD), F32),
        vmem((NB, X * group, HD), F32),
        vmem((Y, Z, CAP, wa), BF),
        vmem((X, Z, CAP, wb), BF),
        vmem((max(Y - 1, 1), Z, CAP, wa), BF),
        vmem((max(X - 1, 1), Z, CAP, wb), BF),
        vmem((Z, CAP, wa), BF),
        vmem((Z, CAP, wb), BF),
        vmem((Z - 1, CAP, wa), BF),
        vmem((Z - 1, CAP, wb), BF),
        vmem((Z, CAP, feat), BF),
        vmem((2, H // 2, group + CAP, HD), BF),
        vmem((H // 2, group + CAP, HD), BF),
        vmem((H // 2, group + CAP, HD), BF),
        vmem((max(H // 2 - 1, 1), group + CAP, HD), BF),
        vmem((Z, CAP, 2 * HD), BF),
        vmem((Z - 1, CAP, 2 * HD), BF),
        vmem((tok, feat), BF),
        vmem((Z, 2 * HD, feat), BF),
        pltpu.SemaphoreType.DMA((n_copies,)),
        pltpu.SemaphoreType.DMA((n_copies,)),
        pltpu.SemaphoreType.DMA((9,)),
    ]
    return pl.pallas_call(
        body,
        out_shape=jax.ShapeDtypeStruct((tok, feat), BF),
        in_specs=[pl.BlockSpec(memory_space=pl.ANY)] * 7,
        out_specs=pl.BlockSpec(memory_space=pltpu.VMEM),
        scratch_shapes=scratch,
        compiler_params=pltpu.CompilerParams(
            collective_id=0, has_side_effects=True, vmem_limit_bytes=60 * 2**20
        ),
    )(queries, keys, values, hidden, cached, active.reshape(1, tok), w_out.T)


def solution(mesh):
    placed = (
        P("seq", "head"),
        P("seq", "head"),
        P("seq", "head"),
        P("seq", "head"),
        P("seq", "head"),
        P("seq"),
        P("head", "seq"),
    )
    return jax.shard_map(
        shards, mesh=mesh, in_specs=placed, out_specs=P("seq", "head"), check_vma=False
    )
```
